256 devices in a mesh: pipe: 4 (over z_hi), expert: 64 (over y, z_lo, x, core).
Axes of the slice: x: 4, y: 4, z: 8 (z_hi: 4, z_lo: 2; z = z_hi * 2 + z_lo), core: 2. Of those that a mesh axis runs over, the one named last changes fastest.
Arguments:
- forward_rows: bfloat16 [4, 4096, 3584], P('pipe', 'expert'), may hold values from -6 to 6
- forward_routes: int32 [4, 4096, 2], P('pipe', 'expert'), may hold values from 0 to 31, all different within a row; in each aligned block of 64 rows (0 to 63, 64 to 127, ..., all dimensions but the last counted through in order) at most 5 rows name the same one
- saved_rows: bfloat16 [4, 4096, 3584], P('pipe', 'expert'), may hold values from -6 to 6
- cotangent: bfloat16 [4, 4096, 3584], P('pipe', 'expert'), may hold values from -6 to 6
- backward_routes: int32 [4, 4096, 2], P('pipe', 'expert'), may hold values from 0 to 31, all different within a row; in each aligned block of 64 rows (0 to 63, 64 to 127, ..., all dimensions but the last counted through in order) at most 5 rows name the same one
- norm_gain: float32 [4, 3584], P('pipe'), may hold values from 0.1 to 1.9
- router: bfloat16 [4, 3584, 32], P('pipe'), may hold values from -0.09375 to 0.09375
- gate_weight: bfloat16 [4, 64, 3584, 512], P('pipe', 'expert'), may hold values from -0.09375 to 0.09375
- up_weight: bfloat16 [4, 64, 3584, 512], P('pipe', 'expert'), may hold values from -0.09375 to 0.09375
- down_weight: bfloat16 [4, 64, 512, 3584], P('pipe', 'expert'), may hold values from -0.1875 to 0.1875
Outputs:
- forward_next: bfloat16 [4, 4096, 3584], P('pipe', 'expert')
- backward_next: bfloat16 [4, 4096, 3584], P('pipe', 'expert')
The draws below stay inside these ranges and needn't reach their ends.
Inputs may be any that keep to these rules, and one draw needn't show every extreme that they name: `forward_routes`: each row names 2 different experts. Within the rows of one device (aligned blocks of 64 rows) no expert is named more than 5 times, a bound that some block reaches. `backward_routes`: as forward_routes.
All inputs are finite; a program needn't handle non-finite values.
Results may differ from the reference program's by a relative error of at most 0.007.
Values may be sent and summed in bfloat16 or wider, within the bound.
No kernel may reach another device: no remote copies, remote signals or barrier semaphores. Data moves between devices by JAX's collectives and lax.ppermute only.
A program may use at most 128 MiB of HBM per device.

```python
import math
import jax
import jax.numpy as jnp
import numpy as np
from jax import lax

D = 3584
H = 1024
H_DEV = 512
TOP = 2
TOK_DEV = 64
SPLIT = 2
EXPERTS = 32
CAP = 5
TOKENS = 4096
N_PIPE = 4
N_EXPERT = 64


def block_scale(stream_key, extent, cuts, low, largest):
    gain, own = 1.0, jax.random.fold_in(stream_key, 6)
    for dim, shards_of in cuts:
        draws = jnp.exp(jax.random.uniform(jax.random.fold_in(own, dim), (shards_of,), jnp.float32, low / len(cuts), largest / len(cuts)))
        gain = gain * jnp.repeat(draws, extent[dim] // shards_of).reshape([-1 if axis == dim else 1 for axis in range(len(extent))])
    return gain


def routed_block(stream_key, own, number, rows, count, top, most, lean):
    order = jax.random.permutation(stream_key, count)
    packed, usual = shares(count, rows * top, most, lean, True), shares(count, rows * top, most, lean, False)
    places = jnp.arange(count)

    def named(tallies, turn):
        used = int((tallies > 0).sum())
        fixed = max(1, used // 4)
        shifted = fixed + (places - fixed + turn * (used - fixed)) % max(1, count - fixed)
        return jnp.zeros((count,), jnp.int32).at[order[jnp.where(places < fixed, places, shifted)]].set(jnp.asarray(tallies, jnp.int32))

    tallies = jnp.where(number % 4 == 0, named(packed, number // 4), named(usual, number - number // 4 - 1))
    mixed = jax.random.permutation(jax.random.fold_in(own, 3), count)
    donor, taker = mixed[0:count // 2 * 2:2], mixed[1:count // 2 * 2:2]
    margin = jnp.minimum(tallies[donor] - 1, most - tallies[taker]) // 2
    margin = jnp.where((donor == order[0]) | (taker == order[0]) | (tallies[taker] == 0), 0, jnp.maximum(margin, 0))
    shifted = jax.random.randint(jax.random.fold_in(own, 4), (count // 2,), 0, 1 << 20) % (margin + 1)
    tallies = tallies.at[donor].add(-shifted).at[taker].add(shifted)
    labels = jnp.searchsorted(jnp.cumsum(tallies), jnp.arange(rows * top), side="right").astype(jnp.int32)
    table = labels.reshape(top, rows).T
    table = table[jax.random.permutation(jax.random.fold_in(own, 1), rows)]
    turn = jax.random.randint(jax.random.fold_in(own, 2), (rows, 1), 0, top)
    return jnp.take_along_axis(table, (jnp.arange(top)[None, :] + turn) % top, axis=1)


def shares(amount, total, limit, skew, full):
    portions = [(1 << 20) // math.isqrt(grade ** skew) + 1 for grade in range(1, amount + 1)]
    largest = limit if full else min(limit, max(-(-total // amount), total * portions[0] // sum(portions)))
    least = 1 if total - largest >= amount - 1 else 0
    given, spare = [largest] + [least] * (amount - 1), total - largest - least * (amount - 1)
    while spare > 0:
        free = [i for i in range(1, amount) if given[i] < largest] or [i for i in range(1, amount) if given[i] < limit]
        mass, left = sum([portions[i] for i in free]), spare
        for i in free:
            addition = min(limit - given[i], max(1, left * portions[i] // mass), spare)
            given[i] = given[i] + addition
            spare = spare - addition
    return np.array(given)


def scatter_about(own_key, shape, width, reach, split=(), kind=jnp.bfloat16):
    drawn = jax.random.normal(own_key, shape, jnp.float32) * width
    if len(split) > 0:
        drawn = block_scale(own_key, shape, split, -0.22, 0.18) * drawn
    return jnp.clip(drawn, min=-reach, max=reach).astype(kind)


def setup_inputs(seed: int = 0) -> dict:
    splits = jax.random.split(jax.random.key(seed), 11)
    forward_rows = scatter_about(splits[0], (N_PIPE, TOKENS, D), 1.0, 6.0, ((0, 4), (1, 64)))
    forward_routes_keys = jax.random.split(jax.random.fold_in(splits[1], 1), N_PIPE * TOKENS // TOK_DEV)
    forward_routes_turns = jax.random.permutation(jax.random.fold_in(splits[1], 3), N_PIPE * TOKENS // TOK_DEV)
    forward_routes = jax.vmap(lambda own, number: routed_block(jax.random.fold_in(splits[1], 2), own, number, TOK_DEV, EXPERTS, TOP, CAP, 1))(forward_routes_keys, forward_routes_turns).reshape((N_PIPE, TOKENS, TOP))
    saved_rows = scatter_about(splits[2], (N_PIPE, TOKENS, D), 1.0, 6.0, ((0, 4), (1, 64)))
    cotangent = scatter_about(splits[3], (N_PIPE, TOKENS, D), 1.0, 6.0, ((0, 4), (1, 64)))
    backward_routes_keys = jax.random.split(jax.random.fold_in(splits[4], 1), N_PIPE * TOKENS // TOK_DEV)
    backward_routes_turns = jax.random.permutation(jax.random.fold_in(splits[4], 3), N_PIPE * TOKENS // TOK_DEV)
    backward_routes = jax.vmap(lambda own, number: routed_block(jax.random.fold_in(splits[4], 2), own, number, TOK_DEV, EXPERTS, TOP, CAP, 1))(backward_routes_keys, backward_routes_turns).reshape((N_PIPE, TOKENS, TOP))
    norm_gain = jnp.clip(1.0 + 0.18 * jax.random.normal(splits[5], (N_PIPE, D), jnp.float32), 0.1, 1.9)
    router = scatter_about(splits[6], (N_PIPE, D, EXPERTS), D ** -0.5, 0.09375, ((0, 4),))
    gate_weight = scatter_about(splits[7], (N_PIPE, SPLIT * EXPERTS, D, H_DEV), D ** -0.5, 0.09375, ((0, 4), (1, 64)))
    up_weight = scatter_about(splits[8], (N_PIPE, SPLIT * EXPERTS, D, H_DEV), D ** -0.5, 0.09375, ((0, 4), (1, 64)))
    down_weight = scatter_about(splits[9], (N_PIPE, SPLIT * EXPERTS, H_DEV, D), H ** -0.5, 0.1875, ((0, 4), (1, 64)))
    return {"forward_rows": forward_rows, "forward_routes": forward_routes, "saved_rows": saved_rows, "cotangent": cotangent, "backward_routes": backward_routes, "norm_gain": norm_gain, "router": router, "gate_weight": gate_weight, "up_weight": up_weight, "down_weight": down_weight}


epsilon = 1e-06

def prepare(values, norm_gain_row, router_map, routes):
    inverse = lax.rsqrt(lax.optimization_barrier(jnp.mean(values * values, axis=-1, keepdims=True)) + epsilon)
    normed = values * inverse * norm_gain_row
    logits = jnp.dot(normed, router_map.astype(jnp.float32), precision=lax.Precision.HIGHEST)
    scores = jax.nn.sigmoid(logits)
    choices_axis = jnp.arange(router_map.shape[1], dtype=jnp.int32)
    onehot = (routes[:, :, None] == choices_axis[None, None, :]).astype(scores.dtype)
    picked = lax.optimization_barrier(jnp.sum(onehot * scores[:, None, :], axis=-1))
    return (normed, picked / lax.optimization_barrier(jnp.sum(picked, axis=1, keepdims=True)))

def slot_of(routes, experts):
    flat_routes = routes.reshape(-1)
    onehot = (flat_routes[:, None] == jnp.arange(experts, dtype=jnp.int32)[None, :]).astype(jnp.int32)
    before = jnp.cumsum(onehot, axis=0) - onehot
    return lax.optimization_barrier(jnp.sum(before * onehot, axis=1)).reshape(routes.shape)

def expert_forward(activation, w_gate, w_up, w_down):
    gate_out = jnp.dot(activation, w_gate, preferred_element_type=jnp.float32)
    upper = jnp.dot(activation, w_up, preferred_element_type=jnp.float32)
    hidden = (jax.nn.silu(gate_out) * upper).astype(jnp.bfloat16)
    return jnp.dot(hidden, w_down, preferred_element_type=jnp.float32).astype(jnp.bfloat16)

def expert_backward(activation, cotan_rows, w_gate, w_up, w_down):
    contract = (((1,), (1,)), ((), ()))
    gate_out = jnp.dot(activation, w_gate, preferred_element_type=jnp.float32)
    upper = jnp.dot(activation, w_up, preferred_element_type=jnp.float32)
    sigmoid_gate = jax.nn.sigmoid(gate_out)
    active = gate_out * sigmoid_gate
    hidden = (active * upper).astype(jnp.bfloat16)
    partial_value = jnp.dot(hidden, w_down, preferred_element_type=jnp.float32).astype(jnp.bfloat16)
    inner_dot = lax.optimization_barrier(jnp.sum(partial_value.astype(jnp.float32) * cotan_rows.astype(jnp.float32), axis=-1)).astype(jnp.bfloat16)
    d_hidden = lax.dot_general(cotan_rows, w_down, contract, preferred_element_type=jnp.float32)
    d_gate = (d_hidden * upper * sigmoid_gate * (1.0 + gate_out * (1.0 - sigmoid_gate))).astype(jnp.bfloat16)
    d_up = (d_hidden * active).astype(jnp.bfloat16)
    back_rows = lax.dot_general(d_gate, w_gate, contract, preferred_element_type=jnp.float32)
    back_rows = back_rows + lax.dot_general(d_up, w_up, contract, preferred_element_type=jnp.float32)
    return (back_rows.astype(jnp.bfloat16), inner_dot)

def place(values, routes):
    blocks = routes.reshape(N_EXPERT, TOK_DEV, TOP)
    slots = jax.vmap(lambda block_ids: slot_of(block_ids, EXPERTS))(blocks).reshape(TOKENS, TOP)
    source = (jnp.arange(TOKENS, dtype=jnp.int32) // TOK_DEV)[:, None]
    lookup = routes * (N_EXPERT * CAP) + source * CAP + slots
    spread = jnp.broadcast_to(values[:, None, :], (TOKENS, TOP, D)).reshape(TOKENS * TOP, D)
    buffer = jnp.zeros((EXPERTS * N_EXPERT * CAP, D), values.dtype).at[lookup.reshape(-1)].set(spread)
    return (buffer.reshape(EXPERTS, N_EXPERT * CAP, D), lookup)

def arrange(weight_stack):
    shaped = weight_stack.reshape((SPLIT, EXPERTS) + weight_stack.shape[1:])
    return jnp.swapaxes(shaped, 0, 1)

def section_forward(activation, routes, gain_row, router_map, gate_stack, up_stack, down_stack):
    normed, weights = prepare(activation.astype(jnp.float32), gain_row, router_map, routes)
    buffer, lookup = place(normed.astype(jnp.bfloat16), routes)

    def one_expert(operands):
        block_rows, gates, uppers, downs = operands
        summed = jnp.zeros(block_rows.shape, jnp.float32)
        for portion in range(SPLIT):
            summed = summed + expert_forward(block_rows, gates[portion], uppers[portion], downs[portion]).astype(jnp.float32)
        return summed
    outputs = lax.map(one_expert, (buffer, arrange(gate_stack), arrange(up_stack), arrange(down_stack))).reshape(-1, D)
    picked = outputs[lookup]
    mixture = lax.optimization_barrier(jnp.sum(weights[:, :, None] * picked, axis=1))
    return (activation.astype(jnp.float32) + mixture).astype(jnp.bfloat16)

def section_backward(activation, cotan_rows, routes, gain_row, router_map, gate_stack, up_stack, down_stack):
    (normed, weights), pullback = jax.vjp(lambda vector: prepare(vector, gain_row, router_map, routes), activation.astype(jnp.float32))
    buffer, lookup = place(normed.astype(jnp.bfloat16), routes)
    cot_buffer, lookup_again = place(cotan_rows, routes)

    def one_expert(operands):
        block_rows, block_cot, gates, uppers, downs = operands
        summed = jnp.zeros(block_rows.shape, jnp.float32)
        inner_sum = jnp.zeros(block_rows.shape[:1], jnp.float32)
        for portion in range(SPLIT):
            back_rows, inner_dot = expert_backward(block_rows, block_cot, gates[portion], uppers[portion], downs[portion])
            summed = summed + back_rows.astype(jnp.float32)
            inner_sum = inner_sum + inner_dot.astype(jnp.float32)
        return (summed, inner_sum)
    backs, inners = lax.map(one_expert, (buffer, cot_buffer, arrange(gate_stack), arrange(up_stack), arrange(down_stack)))
    picked = backs.reshape(-1, D)[lookup]
    inner_picked = inners.reshape(-1)[lookup]
    d_normed = lax.optimization_barrier(jnp.sum(weights[:, :, None] * picked, axis=1))
    d_rows, = pullback((d_normed, inner_picked))
    return (cotan_rows.astype(jnp.float32) + d_rows).astype(jnp.bfloat16)

def reference(forward_rows, forward_routes, saved_rows, cotangent, backward_routes, norm_gain, router, gate_weight, up_weight, down_weight):
    outputs = []
    grads = []
    for section in range(N_PIPE):
        outputs.append(section_forward(forward_rows[section], forward_routes[section], norm_gain[section], router[section], gate_weight[section], up_weight[section], down_weight[section]))
        grads.append(section_backward(saved_rows[section], cotangent[section], backward_routes[section], norm_gain[section], router[section], gate_weight[section], up_weight[section], down_weight[section]))
    forward_next = jnp.roll(jnp.stack(outputs), 1, axis=0)
    backward_next = jnp.roll(jnp.stack(grads), -1, axis=0)
    return (forward_next, backward_next)
```

```python
import itertools

import jax
import jax.numpy as jnp
import numpy as np
from jax import lax
from jax.experimental import pallas as pl
from jax.experimental.pallas import tpu as pltpu
from jax.sharding import PartitionSpec as P

epsilon = 1e-06
SIZES = {"y": 4, "z": 2, "x": 4, "c": 2}
PLACE = {"z": 0, "x": 1, "c": 2, "y": 3}
CAP = 5
LABELS = list(itertools.product(range(2), range(4), range(2), range(2), range(CAP)))


def split_labels(axis):
    at = PLACE[axis]
    count = 2 if axis == "y" else SIZES[axis]
    return [[label for label in LABELS if label[at] == k] for k in range(count)]


def moved(x, axis, by):
    pairs = []
    for y, z, x_, c in itertools.product(range(4), range(2), range(4), range(2)):
        at = {"y": y, "z": z, "x": x_, "c": c}
        to = dict(at)
        to[axis] = (at[axis] + by) % SIZES[axis]
        pairs.append(
            (
                ((at["y"] * 2 + at["z"]) * 4 + at["x"]) * 2 + at["c"],
                ((to["y"] * 2 + to["z"]) * 4 + to["x"]) * 2 + to["c"],
            )
        )
    return lax.ppermute(x, "expert", pairs)


def passed_along(x, axis, by):
    count = lax.axis_size(axis)
    return lax.ppermute(x, axis, [(i, (i + by) % count) for i in range(count)])


def chunk_of(width):
    for size in (512, 384, 256, 128):
        if width % size == 0:
            return size
    return width


def mix_rows(arrays, mats, out_rows, out_dtype=jnp.bfloat16):
    width = arrays[0].shape[1]
    keys = sorted(mats)
    size = chunk_of(width)
    n_in, n_mat = len(arrays), len(keys)

    def kernel(*refs):
        ins, ms, outs = refs[:n_in], refs[n_in : n_in + n_mat], refs[n_in + n_mat :]

        def step(n, carry):
            cols = pl.ds(pl.multiple_of(n * size, 128), size)
            for k in range(len(outs)):
                total = None
                for (kk, i), m in zip(keys, ms):
                    if kk != k:
                        continue
                    term = jnp.dot(m[...], ins[i][:, cols], preferred_element_type=jnp.float32)
                    total = term if total is None else total + term
                outs[k][:, cols] = total.astype(outs[k].dtype)
            return carry

        lax.fori_loop(0, width // size, step, 0)

    ops = sum(2 * mats[key].shape[0] * mats[key].shape[1] * width for key in keys)
    moved_bytes = sum(a.shape[0] for a in arrays) * width * 2 + sum(out_rows) * width * 2
    return pl.pallas_call(
        kernel,
        out_shape=[jax.ShapeDtypeStruct((rows, width), out_dtype) for rows in out_rows],
        in_specs=[pl.BlockSpec(memory_space=pltpu.VMEM)] * (n_in + n_mat),
        out_specs=[pl.BlockSpec(memory_space=pltpu.VMEM)] * len(out_rows),
        compiler_params=pltpu.CompilerParams(vmem_limit_bytes=32 * 1024 * 1024),
        cost_estimate=pl.CostEstimate(flops=ops, bytes_accessed=moved_bytes, transcendentals=0),
    )(*arrays, *[mats[key] for key in keys])


def regroup(pieces, out_labels):
    mats = {}
    for k, wanted in enumerate(out_labels):
        for i, (_, labels) in enumerate(pieces):
            m = np.array([[float(a == b) for b in labels] for a in wanted])
            if m.any():
                mats[(k, i)] = jnp.asarray(m, jnp.bfloat16)
    return mix_rows([a for a, _ in pieces], mats, [len(labels) for labels in out_labels])


def exchange(outs, axis, sign):
    return [
        (out if k == 0 else moved(out, axis, sign * k), labels)
        for k, (out, labels) in enumerate(zip(outs, split_labels(axis)))
    ]


def label_expert(label, me):
    y, z, x, c = me
    rz, rx, rc, ry, _ = label
    return rz, rx, rc, ry


def row_tables(labels, me):
    y, z, x, c = me
    columns = np.array(labels, np.int32)
    rz, rx, rc, ry, s = (jnp.asarray(columns[:, i]) for i in range(5))
    expert = (
        ((((y % 2) + ry) % 2) * 2 + (z + rz) % 2) * 4 + (x + rx) % 4
    ) * 2 + (c + rc) % 2
    return expert, s


def slot_of(routes, experts):
    flat = routes.T.reshape(-1)
    onehot = (flat[:, None] == jnp.arange(experts, dtype=jnp.int32)[None, :]).astype(jnp.bfloat16)
    n = flat.shape[0]
    lower = jnp.asarray(np.tril(np.ones((n, n)), -1), jnp.bfloat16)
    before = jnp.dot(lower, onehot, preferred_element_type=jnp.float32)
    slots = jnp.sum(before * onehot.astype(jnp.float32), axis=1).astype(jnp.int32)
    return slots.reshape(routes.shape[1], routes.shape[0]).T


def match_in(ids, slots, labels, me):
    expert, s = row_tables(labels, me)
    hit = (ids.T[:, None, :] == expert[None, :, None]) & (slots.T[:, None, :] == s[None, :, None])
    return jnp.any(hit, axis=0).astype(jnp.bfloat16)


def match_out(ids, slots, labels, me):
    expert, s = row_tables(labels, me)
    hit = (ids[:, :, None] == expert[None, None, :]) & (slots[:, :, None] == s[None, None, :])
    return hit.astype(jnp.float32)


def dispatch(rows, ids, slots, me, order):
    groups = split_labels(order[0])
    mats = {(k, 0): match_in(ids, slots, labels, me) for k, labels in enumerate(groups)}
    outs = mix_rows([rows], mats, [len(labels) for labels in groups])
    pieces = exchange(outs, order[0], 1)
    for axis in order[1:]:
        pieces = exchange(regroup(pieces, split_labels(axis)), axis, 1)
    same, other = regroup(pieces, split_labels("y"))
    return [same, moved(other, "y", 1), moved(same, "y", 2), moved(other, "y", -1)]


def collect(results, order):
    same, other = split_labels("y")
    pieces = [
        (results[0], same),
        (moved(results[2], "y", 2), same),
        (moved(results[1], "y", -1), other),
        (moved(results[3], "y", 1), other),
    ]
    for axis in order:
        pieces = exchange(regroup(pieces, split_labels(axis)), axis, -1)
    return pieces


def combine(pieces, weights, ids, slots, me):
    mats = {}
    for i, (_, labels) in enumerate(pieces):
        spread = jnp.sum(weights[:, :, None] * match_out(ids, slots, labels, me), axis=1)
        high = spread.astype(jnp.bfloat16)
        low = (spread - high.astype(jnp.float32)).astype(jnp.bfloat16)
        mats[(0, 2 * i)] = high
        mats[(0, 2 * i + 1)] = low
    merged = {}
    for (k, i), m in mats.items():
        merged[(0, i)] = m
    return mix_twice([a for a, _ in pieces], merged)


def mix_twice(arrays, mats):
    width = arrays[0].shape[1]
    size = chunk_of(width)
    rows = mats[(0, 0)].shape[0]
    n = len(arrays)

    def kernel(*refs):
        ins, ms, out = refs[:n], refs[n : 3 * n], refs[3 * n]

        def step(at, carry):
            cols = pl.ds(pl.multiple_of(at * size, 128), size)
            total = jnp.zeros((rows, size), jnp.float32)
            for i in range(n):
                block = ins[i][:, cols]
                total += jnp.dot(ms[2 * i][...], block, preferred_element_type=jnp.float32)
                total += jnp.dot(ms[2 * i + 1][...], block, preferred_element_type=jnp.float32)
            out[:, cols] = total
            return carry

        lax.fori_loop(0, width // size, step, 0)

    held = sum(a.shape[0] for a in arrays)
    return pl.pallas_call(
        kernel,
        out_shape=jax.ShapeDtypeStruct((rows, width), jnp.float32),
        in_specs=[pl.BlockSpec(memory_space=pltpu.VMEM)] * (3 * n),
        out_specs=pl.BlockSpec(memory_space=pltpu.VMEM),
        compiler_params=pltpu.CompilerParams(vmem_limit_bytes=32 * 1024 * 1024),
        cost_estimate=pl.CostEstimate(
            flops=4 * rows * held * width,
            bytes_accessed=held * width * 2 + rows * width * 4,
            transcendentals=0,
        ),
    )(*arrays, *[mats[(0, i)] for i in range(2 * n)])


def normalise(values, gain_row):
    inverse = lax.rsqrt(jnp.mean(values * values, axis=-1, keepdims=True) + epsilon)
    return values * inverse * gain_row


def gates(normed, router_map, routes):
    logits = jnp.dot(normed, router_map.astype(jnp.float32), precision=lax.Precision.HIGHEST)
    scores = jax.nn.sigmoid(logits)
    choices_axis = jnp.arange(router_map.shape[1], dtype=jnp.int32)
    onehot = (routes[:, :, None] == choices_axis[None, None, :]).astype(scores.dtype)
    picked = jnp.sum(onehot * scores[:, None, :], axis=-1)
    return picked / jnp.sum(picked, axis=1, keepdims=True)


def expert_forward(activation, w_gate, w_up, w_down):
    gate_out = jnp.dot(activation, w_gate, preferred_element_type=jnp.float32)
    upper = jnp.dot(activation, w_up, preferred_element_type=jnp.float32)
    hidden = (jax.nn.silu(gate_out) * upper).astype(jnp.bfloat16)
    return jnp.dot(hidden, w_down, preferred_element_type=jnp.float32).astype(jnp.bfloat16)


def expert_backward(activation, cotan_rows, w_gate, w_up, w_down):
    contract = (((1,), (1,)), ((), ()))
    gate_out = jnp.dot(activation, w_gate, preferred_element_type=jnp.float32)
    upper = jnp.dot(activation, w_up, preferred_element_type=jnp.float32)
    sigmoid_gate = jax.nn.sigmoid(gate_out)
    active = gate_out * sigmoid_gate
    hidden = (active * upper).astype(jnp.bfloat16)
    partial_value = jnp.dot(hidden, w_down, preferred_element_type=jnp.float32).astype(jnp.bfloat16)
    inner_dot = jnp.sum(
        partial_value.astype(jnp.float32) * cotan_rows.astype(jnp.float32), axis=-1
    ).astype(jnp.bfloat16)
    d_hidden = lax.dot_general(cotan_rows, w_down, contract, preferred_element_type=jnp.float32)
    d_gate = (d_hidden * upper * sigmoid_gate * (1.0 + gate_out * (1.0 - sigmoid_gate))).astype(
        jnp.bfloat16
    )
    d_up = (d_hidden * active).astype(jnp.bfloat16)
    back_rows = lax.dot_general(d_gate, w_gate, contract, preferred_element_type=jnp.float32)
    back_rows = back_rows + lax.dot_general(
        d_up, w_up, contract, preferred_element_type=jnp.float32
    )
    return (back_rows.astype(jnp.bfloat16), inner_dot)


def body(
    forward_rows,
    forward_routes,
    saved_rows,
    cotangent,
    backward_routes,
    norm_gain,
    router,
    gate_weight,
    up_weight,
    down_weight,
):
    experts = router.shape[2]
    number = lax.axis_index("expert")
    me = (number // 16, (number // 8) % 2, (number // 2) % 4, number % 2)
    gain_row, router_map = norm_gain[0], router[0]
    w_gate, w_up, w_down = gate_weight[0, 0], up_weight[0, 0], down_weight[0, 0]
    model_width = w_gate.shape[0]

    backward_ids = backward_routes[0]
    backward_slots = slot_of(backward_ids, experts)
    cotan_input = cotangent[0]
    saved_input = saved_rows[0].astype(jnp.float32)
    backward_normed, norm_back = jax.vjp(lambda v: normalise(v, gain_row), saved_input)
    rows_in = dispatch(
        backward_normed.astype(jnp.bfloat16), backward_ids, backward_slots, me, ("z", "x", "c")
    )
    cotan_in = dispatch(cotan_input, backward_ids, backward_slots, me, ("x", "z", "c"))

    forward_ids = forward_routes[0]
    forward_slots = slot_of(forward_ids, experts)
    forward_input = forward_rows[0].astype(jnp.float32)
    forward_normed = normalise(forward_input, gain_row)
    forward_in = dispatch(
        forward_normed.astype(jnp.bfloat16), forward_ids, forward_slots, me, ("z", "x", "c")
    )
    backward_weights, gate_back = jax.vjp(
        lambda n: gates(n, router_map, backward_ids), backward_normed
    )
    forward_weights = gates(forward_normed, router_map, forward_ids)

    back_rows, inner_dot = expert_backward(
        jnp.concatenate(rows_in), jnp.concatenate(cotan_in), w_gate, w_up, w_down
    )
    wide = jnp.concatenate(
        [back_rows, jnp.broadcast_to(inner_dot[:, None], (back_rows.shape[0], 128))], axis=1
    )
    back_pieces = collect(jnp.split(wide, 4), ("c", "x", "z"))

    partial_rows = expert_forward(jnp.concatenate(forward_in), w_gate, w_up, w_down)
    forward_pieces = collect(jnp.split(partial_rows, 4), ("c", "x", "z"))

    d_wide = combine(back_pieces, backward_weights, backward_ids, backward_slots, me)
    d_normed = d_wide[:, :model_width]
    inner = sum(
        jnp.sum(
            match_out(backward_ids, backward_slots, labels, me)
            * piece[:, model_width].astype(jnp.float32)[None, None, :],
            axis=-1,
        )
        for piece, labels in back_pieces
    )
    (d_from_gates,) = gate_back(inner)
    (d_rows,) = norm_back(d_normed + d_from_gates)
    gradient = (cotan_input.astype(jnp.float32) + d_rows).astype(jnp.bfloat16)
    backward_next = passed_along(gradient[None], "pipe", -1)

    mixture = combine(forward_pieces, forward_weights, forward_ids, forward_slots, me)
    result = (forward_input + mixture).astype(jnp.bfloat16)
    forward_next = passed_along(result[None], "pipe", 1)
    return (forward_next, backward_next)


def solution(mesh):
    in_specs = (
        P("pipe", "expert", None),
        P("pipe", "expert", None),
        P("pipe", "expert", None),
        P("pipe", "expert", None),
        P("pipe", "expert", None),
        P("pipe", None),
        P("pipe", None, None),
        P("pipe", "expert", None, None),
        P("pipe", "expert", None, None),
        P("pipe", "expert", None, None),
    )
    out_specs = (P("pipe", "expert", None), P("pipe", "expert", None))
    return jax.shard_map(body, mesh=mesh, in_specs=in_specs, out_specs=out_specs, check_vma=False)
```

```python
import jax
import jax.numpy as jnp
import numpy as np
from jax import lax
from jax.experimental import pallas as pl
from jax.experimental.pallas import tpu as pltpu
from jax.sharding import PartitionSpec as P

epsilon = 1e-06
VMEM_LIMIT = 32 * 1024 * 1024
CAP = 5
LANES = 1152
ROWS = 16
TAIL = 3 * LANES
FAR = pl.BlockSpec(memory_space=pltpu.HBM)
NEAR = pl.BlockSpec(memory_space=pltpu.VMEM)


def selections():
    body = np.zeros((3, 16, CAP, 16, ROWS), np.float32)
    tail = np.zeros((CAP, 16, CAP, 16, ROWS), np.float32)
    for i in range(16):
        for s in range(CAP):
            tail[s, i, s, i, 15] = 1
            for g in range(3):
                body[g, i, s, i, 5 * g + s] = 1
    body, tail = body.reshape(240, 256), tail.reshape(400, 256)
    gather = np.concatenate([body, tail])
    scatter = np.concatenate([body.T] + [tail[80 * s : 80 * s + 80].T for s in range(CAP)], axis=1)
    scatter = np.concatenate([scatter, tail.reshape(CAP, 80, 256).sum(0).T], axis=1)
    blocks = [scatter[:, :240]] + [scatter[:, 240 + 80 * n : 320 + 80 * n] for n in range(CAP + 1)]
    scatter = np.concatenate([np.pad(b, ((0, 0), (0, 240 - b.shape[1]))) for b in blocks])
    return jnp.asarray(gather, jnp.bfloat16), jnp.asarray(scatter, jnp.bfloat16)


def params():
    return dict(
        compiler_params=pltpu.CompilerParams(vmem_limit_bytes=VMEM_LIMIT),
        cost_estimate=pl.CostEstimate(flops=0, bytes_accessed=1024, transcendentals=0),
    )


def f32(x):
    return x.astype(jnp.float32)


def count(hits, axis):
    return jnp.sum(jnp.where(hits, 1.0, 0.0), axis=axis, keepdims=True)


def place_of(position):
    expert = lax.bitwise_and(lax.shift_right_logical(position, 4), 31)
    row = lax.bitwise_and(position, 15)
    block = jnp.where(row >= 5, 1, 0) + jnp.where(row >= 10, 1, 0) + jnp.where(row >= 15, 1, 0)
    return expert, row, block, row - 5 * block


def pack(units, gain, ids, after=()):
    n, m = len(units), len(after)
    tokens, width = units[0][0].shape
    half_rows = 32 * ROWS
    ids = ids.astype(jnp.float32)
    ids_rows = jnp.concatenate([ids, ids]).T

    def kernel(*refs):
        rows, (gain_ref, ids_c, ids_r) = refs[:n], refs[n : n + 3]
        out, made, low, high, sems = refs[n + 3 + m :]
        first, second = ids_c[:, 0:1], ids_c[:, 1:2]
        first_r, second_r = ids_r[0:1, :], ids_r[1:2, :]
        shape = (tokens, 2 * tokens)
        token = lax.broadcasted_iota(jnp.int32, shape, 0)
        before = token < lax.bitwise_and(lax.broadcasted_iota(jnp.int32, shape, 1), tokens - 1)
        slot_0 = count((first == first_r) & before, 0)
        slot_1 = count(first == second_r, 0) + count((second == second_r) & before, 0)
        key_0, key_1 = first_r * 8 + slot_0, second_r * 8 + slot_1
        shape = (half_rows, 2 * tokens)
        expert, row, block, slot = place_of(lax.broadcasted_iota(jnp.int32, shape, 0))
        right = lax.broadcasted_iota(jnp.int32, shape, 1) >= tokens

        def hits(key):
            key = f32(key)
            return (key_0 == key) | (key_1 == key)

        def matrix(mask):
            return jnp.where(mask, 1.0, 0.0).astype(jnp.bfloat16)

        own = hits(expert * 8 + slot)
        pick_low = matrix(own & (block == jnp.where(right, 1, 0)))
        third = own & (block == 2) & ~right
        pick_rest = matrix(third)
        picks = [
            matrix(third | (hits(expert * 8 + s) & (row == 15) & right)) for s in range(CAP)
        ]
        for u in range(n):
            x = rows[u][...]
            if units[u][1]:
                v = f32(x)
                inverse = lax.rsqrt(jnp.mean(v * v, axis=-1, keepdims=True) + epsilon)
                x = (v * inverse * gain_ref[...]).astype(jnp.bfloat16)
            low[0:tokens, :] = x[:, :LANES]
            low[tokens:, :] = x[:, LANES : 2 * LANES]
            high[0:tokens, :] = x[:, 2 * LANES : TAIL]
            high[tokens:, :] = jnp.zeros((tokens, LANES), jnp.bfloat16)
            for s in range(CAP):
                high[tokens:, 128 * s : 128 * s + 128] = x[:, TAIL:]
            for s in range(9):
                cols = slice(128 * s, 128 * s + 128)
                part = jnp.dot(pick_low, low[:, cols], preferred_element_type=jnp.float32)
                part += jnp.dot(
                    picks[s] if s < CAP else pick_rest,
                    high[:, cols],
                    preferred_element_type=jnp.float32,
                )
                made[:, u * LANES + 128 * s : u * LANES + 128 * s + 128] = part.astype(
                    jnp.bfloat16
                )
        stores = [
            pltpu.make_async_copy(made, out.at[pl.ds(half_rows * r, half_rows)], sems.at[r])
            for r in range(2)
        ]
        for store in stores:
            store.start()
        for store in stores:
            store.wait()

    return pl.pallas_call(
        kernel,
        out_shape=jax.ShapeDtypeStruct((2 * half_rows, n * LANES), jnp.bfloat16),
        in_specs=[NEAR] * (n + 3) + [pl.BlockSpec(memory_space=pl.ANY)] * m,
        out_specs=FAR,
        scratch_shapes=[
            pltpu.VMEM((half_rows, n * LANES), jnp.bfloat16),
            pltpu.VMEM((2 * tokens, LANES), jnp.bfloat16),
            pltpu.VMEM((2 * tokens, LANES), jnp.bfloat16),
            pltpu.SemaphoreType.DMA((2,)),
        ],
        **params(),
    )(*[rows for rows, _ in units], gain, ids, ids_rows, *after)


def unpack(chunks, gather, x, offset, start):
    def step(b, carry):
        held = pl.ds(pl.multiple_of(256 * b, 256), 256)
        rows = pl.ds(pl.multiple_of(80 * b, 16), 80)
        for c in range(3):
            part = jnp.dot(
                gather[:240, :],
                chunks[held, offset + 384 * c : offset + 384 * c + 384],
                preferred_element_type=jnp.float32,
            ).astype(jnp.bfloat16)
            for g in range(3):
                at = start + g * LANES + 384 * c
                x[rows, at : at + 384] = part[80 * g : 80 * g + 80]
        total = jnp.zeros((80, 128), jnp.float32)
        for s in range(CAP):
            total += jnp.dot(
                gather[240 + 80 * s : 320 + 80 * s, :],
                chunks[held, offset + 128 * s : offset + 128 * s + 128],
                preferred_element_type=jnp.float32,
            )
        x[rows, start + TAIL : start + TAIL + 128] = total.astype(jnp.bfloat16)
        return carry

    lax.fori_loop(0, 4, step, 0)


def repack(chunks, scatter, made, rest, extra=None):
    def step(b, carry):
        held = pl.ds(pl.multiple_of(256 * b, 256), 256)
        stacked = pl.ds(pl.multiple_of(240 * b, 16), 240)
        rows = pl.ds(pl.multiple_of(80 * b, 16), 80)
        for s in range(9):
            cols = slice(128 * s, 128 * s + 128)
            part = jnp.dot(scatter[:256, :], made[stacked, cols], preferred_element_type=jnp.float32)
            source = rest if s < CAP else extra if s == CAP else None
            if source is not None:
                part += jnp.dot(
                    scatter[256 + 256 * s : 512 + 256 * s, :80],
                    source[rows, :],
                    preferred_element_type=jnp.float32,
                )
            chunks[held, cols] = part.astype(jnp.bfloat16)
        return carry

    lax.fori_loop(0, 4, step, 0)


def put_result(made, rest, product):
    def step(c, carry):
        for g in range(3):
            cols = pl.ds(pl.multiple_of(g * LANES + 384 * c, 128), 384)
            part = product(cols).astype(jnp.bfloat16)
            at = pl.ds(pl.multiple_of(384 * c, 128), 384)
            for b in range(4):
                made[240 * b + 80 * g : 240 * b + 80 * g + 80, at] = part[80 * b : 80 * b + 80]
        return carry

    lax.fori_loop(0, 3, step, 0)
    rest[...] = product(pl.ds(TAIL, 128)).astype(jnp.bfloat16)


def expert_forward(chunks, tables, w_gate, w_up, w_down, after=()):
    width, units = w_gate.shape
    m = len(after)

    def kernel(far, gather, scatter, wg, wu, wd, *refs):
        far_out, near, x, hidden, made, rest, sems = refs[m:]
        load = pltpu.make_async_copy(far, near, sems.at[0])
        load.start()
        load.wait()
        unpack(near, gather, x, 0, 0)

        def first(k, carry):
            cols = pl.ds(pl.multiple_of(k * 256, 256), 256)
            gate = jnp.dot(x[...], wg[:, cols], preferred_element_type=jnp.float32)
            upper = jnp.dot(x[...], wu[:, cols], preferred_element_type=jnp.float32)
            hidden[:, cols] = (gate * jax.nn.sigmoid(gate) * upper).astype(jnp.bfloat16)
            return carry

        lax.fori_loop(0, units // 256, first, 0)
        put_result(
            made,
            rest,
            lambda cols: jnp.dot(hidden[...], wd[:, cols], preferred_element_type=jnp.float32),
        )
        repack(near, scatter, made, rest)
        store = pltpu.make_async_copy(near, far_out, sems.at[1])
        store.start()
        store.wait()

    return pl.pallas_call(
        kernel,
        out_shape=jax.ShapeDtypeStruct(chunks.shape, jnp.bfloat16),
        in_specs=[FAR] + [NEAR] * 5 + [pl.BlockSpec(memory_space=pl.ANY)] * m,
        out_specs=FAR,
        scratch_shapes=[
            pltpu.VMEM(chunks.shape, jnp.bfloat16),
            pltpu.VMEM((320, width), jnp.bfloat16),
            pltpu.VMEM((320, units), jnp.bfloat16),
            pltpu.VMEM((960, LANES), jnp.bfloat16),
            pltpu.VMEM((320, 128), jnp.bfloat16),
            pltpu.SemaphoreType.DMA((2,)),
        ],
        **params(),
    )(chunks, *tables, w_gate, w_up, w_down, *after)


def expert_backward(chunks, tables, w_gate, w_up, w_down):
    width, units = w_gate.shape
    contract = (((1,), (1,)), ((), ()))

    def kernel(far, gather, scatter, wg, wu, wd, far_out, near, x, d_gate, d_up, made, rest, extra, sems):
        load = pltpu.make_async_copy(far, near, sems.at[0])
        load.start()
        load.wait()
        unpack(near, gather, x, 0, 0)
        unpack(near, gather, x, LANES, width)

        def first(k, inner):
            cols = pl.ds(pl.multiple_of(k * 256, 256), 256)
            gate = jnp.dot(x[:, :width], wg[:, cols], preferred_element_type=jnp.float32)
            upper = jnp.dot(x[:, :width], wu[:, cols], preferred_element_type=jnp.float32)
            s = jax.nn.sigmoid(gate)
            d_hidden = lax.dot_general(
                x[:, width:], wd[cols, :], contract, preferred_element_type=jnp.float32
            )
            active = gate * s
            hidden = f32((active * upper).astype(jnp.bfloat16))
            d_gate[:, cols] = (d_hidden * upper * s * (1.0 + gate * (1.0 - s))).astype(
                jnp.bfloat16
            )
            d_up[:, cols] = (d_hidden * active).astype(jnp.bfloat16)
            return inner + jnp.sum(hidden * d_hidden, axis=1, keepdims=True)

        inner = lax.fori_loop(0, units // 256, first, jnp.zeros((320, 1), jnp.float32))
        slot = lax.rem(lax.broadcasted_iota(jnp.int32, (320, 128), 0), CAP)
        lane = lax.broadcasted_iota(jnp.int32, (320, 128), 1)
        extra[...] = jnp.where(slot == lane, inner, 0.0).astype(jnp.bfloat16)

        def product(cols):
            return lax.dot_general(
                d_gate[...], wg[cols, :], contract, preferred_element_type=jnp.float32
            ) + lax.dot_general(
                d_up[...], wu[cols, :], contract, preferred_element_type=jnp.float32
            )

        put_result(made, rest, product)
        repack(near, scatter, made, rest, extra)
        store = pltpu.make_async_copy(near.at[:, pl.ds(0, LANES)], far_out, sems.at[1])
        store.start()
        store.wait()

    return pl.pallas_call(
        kernel,
        out_shape=jax.ShapeDtypeStruct((chunks.shape[0], LANES), jnp.bfloat16),
        in_specs=[FAR] + [NEAR] * 5,
        out_specs=FAR,
        scratch_shapes=[
            pltpu.VMEM(chunks.shape, jnp.bfloat16),
            pltpu.VMEM((320, 2 * width), jnp.bfloat16),
            pltpu.VMEM((320, units), jnp.bfloat16),
            pltpu.VMEM((320, units), jnp.bfloat16),
            pltpu.VMEM((960, LANES), jnp.bfloat16),
            pltpu.VMEM((320, 128), jnp.bfloat16),
            pltpu.VMEM((320, 128), jnp.bfloat16),
            pltpu.SemaphoreType.DMA((2,)),
        ],
        **params(),
    )(chunks, *tables, w_gate, w_up, w_down)


def combine(chunks, weights, ids, base=None):
    tokens = ids.shape[0]
    width = TAIL + 128
    total_rows = chunks.shape[0]
    ids = ids.astype(jnp.float32)
    forward = base is not None

    def kernel(far, w, ids_c, ids_r, *refs):
        if forward:
            base_ref, out, near, parts, tails, sem = refs
        else:
            out, inner_out, near, parts, tails, sem = refs
        load = pltpu.make_async_copy(far, near, sem)
        load.start()
        first, second = ids_c[:, 0:1], ids_c[:, 1:2]
        first_r, second_r = ids_r[0:1, :], ids_r[1:2, :]
        shape = (tokens, tokens)
        before = lax.broadcasted_iota(jnp.int32, shape, 1) < lax.broadcasted_iota(
            jnp.int32, shape, 0
        )
        slot_0 = count((first == first_r) & before, 1)
        slot_1 = count(second == first_r, 1) + count((second == second_r) & before, 1)
        key_0, key_1 = first * 8 + slot_0, second * 8 + slot_1
        shape = (tokens, total_rows)
        expert, row, block, slot = place_of(lax.broadcasted_iota(jnp.int32, shape, 1))

        def spread(key):
            key = f32(key)
            total = jnp.where(key_0 == key, w[:, 0:1], 0.0) + jnp.where(
                key_1 == key, w[:, 1:2], 0.0
            )
            upper = f32(total.astype(jnp.bfloat16))
            return upper, total - upper

        def put(ref, at, values, mask):
            for n, value in enumerate(values):
                ref[at + tokens * n : at + tokens * n + tokens, :] = jnp.where(
                    mask, value, 0.0
                ).astype(jnp.bfloat16)

        values = spread(expert * 8 + slot)
        for g in range(3):
            put(parts, 2 * tokens * g, values, block == g)
        for s in range(CAP):
            put(tails, 2 * tokens * s, spread(expert * 8 + s), row == 15)
        load.wait()
        if not forward:
            lane = f32(lax.broadcasted_iota(jnp.int32, (tokens, 128), 1))
            for k, (chosen, at) in enumerate(((first, slot_0), (second, slot_1))):
                pick = jnp.where((row == 15) & (f32(expert) == chosen), 1.0, 0.0)
                found = jnp.dot(
                    pick.astype(jnp.bfloat16), near[:, 640:768], preferred_element_type=jnp.float32
                )
                inner_out[:, 128 * k : 128 * k + 128] = jnp.broadcast_to(
                    jnp.sum(jnp.where(lane == at, found, 0.0), axis=1, keepdims=True),
                    (tokens, 128),
                )

        def store(at, size, value):
            if forward:
                value = f32(base_ref[:, at : at + size]) + value
            out[:, at : at + size] = value.astype(out.dtype)

        for c in range(3):
            part = jnp.dot(
                parts[...], near[:, 384 * c : 384 * c + 384], preferred_element_type=jnp.float32
            )
            for g in range(3):
                at = 2 * tokens * g
                store(
                    g * LANES + 384 * c,
                    384,
                    part[at : at + tokens] + part[at + tokens : at + 2 * tokens],
                )
        total = jnp.zeros((2 * tokens, 128), jnp.float32)
        for s in range(CAP):
            total += jnp.dot(
                tails[2 * tokens * s : 2 * tokens * (s + 1), :],
                near[:, 128 * s : 128 * s + 128],
                preferred_element_type=jnp.float32,
            )
        store(TAIL, 128, total[:tokens] + total[tokens:])

    outs = [jax.ShapeDtypeStruct((tokens, width), jnp.bfloat16 if forward else jnp.float32)]
    if not forward:
        outs.append(jax.ShapeDtypeStruct((tokens, 256), jnp.float32))
    operands = [weights, ids, ids.T] + ([base] if forward else [])
    return pl.pallas_call(
        kernel,
        out_shape=outs,
        in_specs=[FAR] + [NEAR] * len(operands),
        out_specs=[NEAR] * len(outs),
        scratch_shapes=[
            pltpu.VMEM(chunks.shape, jnp.bfloat16),
            pltpu.VMEM((6 * tokens, total_rows), jnp.bfloat16),
            pltpu.VMEM((2 * CAP * tokens, total_rows), jnp.bfloat16),
            pltpu.SemaphoreType.DMA,
        ],
        **params(),
    )(chunks, *operands)


def swapped(chunks):
    shape = chunks.shape
    chunks = chunks.reshape(shape[0] // ROWS, ROWS, shape[1])
    return lax.all_to_all(chunks, "expert", 0, 0, tiled=True).reshape(shape)


def passed_along(x, axis, by):
    n = lax.axis_size(axis)
    return lax.ppermute(x, axis, [(i, (i + by) % n) for i in range(n)])


def normalise(values, gain_row):
    inverse = lax.rsqrt(jnp.mean(values * values, axis=-1, keepdims=True) + epsilon)
    return values * inverse * gain_row


def gates(normed, router_map, routes):
    logits = jnp.dot(normed, router_map.astype(jnp.float32), precision=lax.Precision.HIGHEST)
    scores = jax.nn.sigmoid(logits)
    choices_axis = jnp.arange(router_map.shape[1], dtype=jnp.int32)
    onehot = (routes[:, :, None] == choices_axis[None, None, :]).astype(scores.dtype)
    picked = jnp.sum(onehot * scores[:, None, :], axis=-1)
    return picked / jnp.sum(picked, axis=1, keepdims=True)


def body(
    forward_rows,
    forward_routes,
    saved_rows,
    cotangent,
    backward_routes,
    norm_gain,
    router,
    gate_weight,
    up_weight,
    down_weight,
):
    gain_row, router_map = norm_gain[0], router[0]
    weights = (gate_weight[0, 0], up_weight[0, 0], down_weight[0, 0])
    tables = selections()
    backward_ids, forward_ids = backward_routes[0], forward_routes[0]

    both_out = pack([(saved_rows[0], True), (cotangent[0], False)], norm_gain, backward_ids)
    forward_out = pack([(forward_rows[0], True)], norm_gain, forward_ids, after=[both_out])
    both_in = swapped(both_out)
    forward_in = swapped(forward_out)
    backward_chunks = expert_backward(both_in, tables, *weights)
    backward_back = swapped(backward_chunks)
    forward_chunks = expert_forward(forward_in, tables, *weights, after=[backward_chunks])
    forward_back = swapped(forward_chunks)

    normed, norm_back = jax.vjp(
        lambda v: normalise(v, gain_row), saved_rows[0].astype(jnp.float32)
    )
    backward_weights, gate_back = jax.vjp(lambda v: gates(v, router_map, backward_ids), normed)
    forward_weights = gates(
        normalise(forward_rows[0].astype(jnp.float32), gain_row), router_map, forward_ids
    )
    d_normed, inner = combine(backward_back, backward_weights, backward_ids)
    (d_from_gates,) = gate_back(jnp.stack([inner[:, 0], inner[:, 128]], axis=1))
    (d_rows,) = norm_back(d_normed + d_from_gates)
    gradient = (cotangent[0].astype(jnp.float32) + d_rows).astype(jnp.bfloat16)
    backward_next = passed_along(gradient[None], "pipe", -1)
    (result,) = combine(forward_back, forward_weights, forward_ids, forward_rows[0])
    forward_next = passed_along(result[None], "pipe", 1)
    return (forward_next, backward_next)


def solution(mesh):
    in_specs = (
        P("pipe", "expert", None),
        P("pipe", "expert", None),
        P("pipe", "expert", None),
        P("pipe", "expert", None),
        P("pipe", "expert", None),
        P("pipe", None),
        P("pipe", None, None),
        P("pipe", "expert", None, None),
        P("pipe", "expert", None, None),
        P("pipe", "expert", None, None),
    )
    out_specs = (P("pipe", "expert", None), P("pipe", "expert", None))
    return jax.shard_map(body, mesh=mesh, in_specs=in_specs, out_specs=out_specs, check_vma=False)
```

```python
import jax
import jax.numpy as jnp
import numpy as np
from jax import lax
from jax.experimental import pallas as pl
from jax.experimental.pallas import tpu as pltpu
from jax.sharding import PartitionSpec as P

epsilon = 1e-06
VMEM_LIMIT = 60 * 1024 * 1024
CAP = 5
LANES = 1152
ROWS = 16
TAIL = 3 * LANES
FAR = pl.BlockSpec(memory_space=pltpu.HBM)
NEAR = pl.BlockSpec(memory_space=pltpu.VMEM)


def selections():
    body = np.zeros((3, 16, CAP, 16, ROWS), np.float32)
    tail = np.zeros((CAP, 16, CAP, 16, ROWS), np.float32)
    for i in range(16):
        for s in range(CAP):
            tail[s, i, s, i, 15] = 1
            for g in range(3):
                body[g, i, s, i, 5 * g + s] = 1
    body, tail = body.reshape(240, 256), tail.reshape(400, 256)
    gather = np.concatenate([body, tail])
    scatter = np.concatenate([body.T] + [tail[80 * s : 80 * s + 80].T for s in range(CAP)], axis=1)
    scatter = np.concatenate([scatter, tail.reshape(CAP, 80, 256).sum(0).T], axis=1)
    blocks = [scatter[:, :240]] + [scatter[:, 240 + 80 * n : 320 + 80 * n] for n in range(CAP + 1)]
    scatter = np.concatenate([np.pad(b, ((0, 0), (0, 240 - b.shape[1]))) for b in blocks])
    return jnp.asarray(gather, jnp.bfloat16), jnp.asarray(scatter, jnp.bfloat16)


def params():
    return dict(
        compiler_params=pltpu.CompilerParams(vmem_limit_bytes=VMEM_LIMIT),
        cost_estimate=pl.CostEstimate(flops=0, bytes_accessed=1024, transcendentals=0),
    )


def f32(x):
    return x.astype(jnp.float32)


def count(hits, axis):
    return jnp.sum(jnp.where(hits, 1.0, 0.0), axis=axis, keepdims=True)


def place_of(position):
    expert = lax.bitwise_and(lax.shift_right_logical(position, 4), 31)
    row = lax.bitwise_and(position, 15)
    block = jnp.where(row >= 5, 1, 0) + jnp.where(row >= 10, 1, 0) + jnp.where(row >= 15, 1, 0)
    return expert, row, block, row - 5 * block


def as_row(column, copies):
    n = column.shape[0]
    shape = (n, copies * n)
    lane = lax.bitwise_and(lax.broadcasted_iota(jnp.int32, shape, 1), n - 1)
    hit = lax.broadcasted_iota(jnp.int32, shape, 0) == lane
    return jnp.sum(jnp.where(hit, column, 0.0), axis=0, keepdims=True)


def pack(units, gain, routes):
    n, m = len(units), len(routes)
    tokens, width = units[0][0].shape
    half_rows = 32 * ROWS
    operands = [*routes, gain, *[rows for rows, _, _ in units]]

    def kernel(*refs):
        far, out = refs[: n + m + 1], refs[n + m + 1]
        near = refs[n + m + 2 : 2 * (n + m) + 3]
        made, low, high, sems = refs[2 * (n + m) + 3 :]
        loads = [
            pltpu.make_async_copy(src, dst, sems.at[i]) for i, (src, dst) in enumerate(zip(far, near))
        ]
        for load in loads:
            load.start()
        for load in loads[: m + 1]:
            load.wait()
        gain_ref = near[m]
        shape = (half_rows, 2 * tokens)
        expert, row, block, slot = place_of(lax.broadcasted_iota(jnp.int32, shape, 0))
        right = lax.broadcasted_iota(jnp.int32, shape, 1) >= tokens
        stores = []
        for route in range(m):
            ids = f32(near[route][...])
            first, second = ids[:, 0:1], ids[:, 1:2]
            first_r, second_r = as_row(first, 2), as_row(second, 2)
            square = (tokens, 2 * tokens)
            lane = lax.bitwise_and(lax.broadcasted_iota(jnp.int32, square, 1), tokens - 1)
            before = lax.broadcasted_iota(jnp.int32, square, 0) < lane
            slot_0 = count((first == first_r) & before, 0)
            slot_1 = count(first == second_r, 0) + count((second == second_r) & before, 0)
            key_0, key_1 = first_r * 8 + slot_0, second_r * 8 + slot_1

            def hits(key, key_0=key_0, key_1=key_1):
                key = f32(key)
                return (key_0 == key) | (key_1 == key)

            def matrix(mask):
                return jnp.where(mask, 1.0, 0.0).astype(jnp.bfloat16)

            own = hits(expert * 8 + slot)
            pick_low = matrix(own & (block == jnp.where(right, 1, 0)))
            third = own & (block == 2) & ~right
            pick_rest = matrix(third)
            picks = [
                matrix(third | (hits(expert * 8 + s) & (row == 15) & right)) for s in range(CAP)
            ]
            for u in range(n):
                if units[u][2] != route:
                    continue
                loads[m + 1 + u].wait()
                x = near[m + 1 + u][...]
                if units[u][1]:
                    v = f32(x)
                    inverse = lax.rsqrt(jnp.mean(v * v, axis=-1, keepdims=True) + epsilon)
                    x = (v * inverse * gain_ref[...]).astype(jnp.bfloat16)
                low[0:tokens, :] = x[:, :LANES]
                low[tokens:, :] = x[:, LANES : 2 * LANES]
                high[0:tokens, :] = x[:, 2 * LANES : TAIL]
                high[tokens:, :] = jnp.zeros((tokens, LANES), jnp.bfloat16)
                for s in range(CAP):
                    high[tokens:, 128 * s : 128 * s + 128] = x[:, TAIL:]
                for s in range(9):
                    cols = slice(128 * s, 128 * s + 128)
                    part = jnp.dot(pick_low, low[:, cols], preferred_element_type=jnp.float32)
                    part += jnp.dot(
                        picks[s] if s < CAP else pick_rest,
                        high[:, cols],
                        preferred_element_type=jnp.float32,
                    )
                    made[:, u * LANES + 128 * s : u * LANES + 128 * s + 128] = part.astype(
                        jnp.bfloat16
                    )
                lanes = pl.ds(u * LANES, LANES)
                for r in range(2):
                    stores.append(
                        pltpu.make_async_copy(
                            made.at[:, lanes],
                            out.at[pl.ds(half_rows * r, half_rows), lanes],
                            sems.at[n + m + 1 + 2 * u + r],
                        )
                    )
                    stores[-1].start()
        for store in stores:
            store.wait()

    return pl.pallas_call(
        kernel,
        out_shape=jax.ShapeDtypeStruct((2 * half_rows, n * LANES), jnp.bfloat16),
        in_specs=[FAR] * (n + m + 1),
        out_specs=FAR,
        scratch_shapes=[pltpu.VMEM(v.shape, v.dtype) for v in operands]
        + [
            pltpu.VMEM((half_rows, n * LANES), jnp.bfloat16),
            pltpu.VMEM((2 * tokens, LANES), jnp.bfloat16),
            pltpu.VMEM((2 * tokens, LANES), jnp.bfloat16),
            pltpu.SemaphoreType.DMA((3 * n + m + 1,)),
        ],
        **params(),
    )(*operands)


def unpack(chunks, gather, x, offset, start):
    def step(b, carry):
        held = pl.ds(pl.multiple_of(256 * b, 256), 256)
        rows = pl.ds(pl.multiple_of(start + 80 * b, 16), 80)
        for c in range(3):
            part = jnp.dot(
                gather[:240, :],
                chunks[held, offset + 384 * c : offset + 384 * c + 384],
                preferred_element_type=jnp.float32,
            ).astype(jnp.bfloat16)
            for g in range(3):
                at = g * LANES + 384 * c
                x[rows, at : at + 384] = part[80 * g : 80 * g + 80]
        total = jnp.zeros((80, 128), jnp.float32)
        for s in range(CAP):
            total += jnp.dot(
                gather[240 + 80 * s : 320 + 80 * s, :],
                chunks[held, offset + 128 * s : offset + 128 * s + 128],
                preferred_element_type=jnp.float32,
            )
        x[rows, TAIL : TAIL + 128] = total.astype(jnp.bfloat16)
        return carry

    lax.fori_loop(0, 4, step, 0)


def repack(chunks, offset, scatter, made, rest, extra=None):
    def step(b, carry):
        held = pl.ds(pl.multiple_of(256 * b, 256), 256)
        stacked = pl.ds(pl.multiple_of(240 * b, 16), 240)
        rows = pl.ds(pl.multiple_of(80 * b, 16), 80)
        for s in range(9):
            cols = slice(128 * s, 128 * s + 128)
            part = jnp.dot(scatter[:256, :], made[stacked, cols], preferred_element_type=jnp.float32)
            source = rest if s < CAP else extra if s == CAP else None
            if source is not None:
                part += jnp.dot(
                    scatter[256 + 256 * s : 512 + 256 * s, :80],
                    source[rows, :],
                    preferred_element_type=jnp.float32,
                )
            chunks[held, offset + 128 * s : offset + 128 * s + 128] = part.astype(jnp.bfloat16)
        return carry

    lax.fori_loop(0, 4, step, 0)


def put_result(made, rest, product):
    def step(c, carry):
        for g in range(3):
            cols = pl.ds(pl.multiple_of(g * LANES + 384 * c, 128), 384)
            part = product(cols).astype(jnp.bfloat16)
            at = pl.ds(pl.multiple_of(384 * c, 128), 384)
            for b in range(4):
                made[240 * b + 80 * g : 240 * b + 80 * g + 80, at] = part[80 * b : 80 * b + 80]
        return carry

    lax.fori_loop(0, 3, step, 0)
    rest[...] = product(pl.ds(TAIL, 128)).astype(jnp.bfloat16)


def experts(chunks, tables, weights):
    width, units = weights[0].shape
    contract = (((1,), (1,)), ((), ()))
    operands = [*tables, *weights]

    def kernel(far, *refs):
        far_in, far_out = refs[:5], refs[5]
        near, gather, scatter, wg, wu, wd, x, cot, hidden, d_gate, d_up, made, rest, extra, sems = (
            refs[6:]
        )
        lanes = [pl.ds(u * LANES, LANES) for u in range(3)]
        parts = [
            pltpu.make_async_copy(far.at[:, lanes[u]], near.at[:, lanes[u]], sems.at[u])
            for u in range(3)
        ]
        tables_in = [
            pltpu.make_async_copy(src, dst, sems.at[3 + n])
            for n, (src, dst) in enumerate(zip(far_in, (gather, scatter, wg, wu, wd)))
        ]
        for load in (tables_in[0], parts[0], parts[2], *tables_in[2:4], parts[1], tables_in[4], tables_in[1]):
            load.start()
        tables_in[0].wait()
        parts[0].wait()
        unpack(near, gather, x, 0, 0)
        parts[2].wait()
        unpack(near, gather, x, 2 * LANES, 320)
        parts[1].wait()
        unpack(near, gather, cot, LANES, 0)
        for load in tables_in[1:]:
            load.wait()

        def first(k, inner):
            cols = pl.ds(pl.multiple_of(k * 256, 256), 256)
            gate = jnp.dot(x[...], wg[:, cols], preferred_element_type=jnp.float32)
            upper = jnp.dot(x[...], wu[:, cols], preferred_element_type=jnp.float32)
            s = jax.nn.sigmoid(gate)
            active = gate * s
            value = (active * upper).astype(jnp.bfloat16)
            hidden[:, cols] = value[320:]
            d_hidden = lax.dot_general(
                cot[...], wd[cols, :], contract, preferred_element_type=jnp.float32
            )
            gate, upper, s, active = gate[:320], upper[:320], s[:320], active[:320]
            d_gate[:, cols] = (d_hidden * upper * s * (1.0 + gate * (1.0 - s))).astype(
                jnp.bfloat16
            )
            d_up[:, cols] = (d_hidden * active).astype(jnp.bfloat16)
            return inner + jnp.sum(f32(value[:320]) * d_hidden, axis=1, keepdims=True)

        inner = lax.fori_loop(0, units // 256, first, jnp.zeros((320, 1), jnp.float32))
        slot = lax.rem(lax.broadcasted_iota(jnp.int32, (320, 128), 0), CAP)
        lane = lax.broadcasted_iota(jnp.int32, (320, 128), 1)
        extra[...] = jnp.where(slot == lane, inner, 0.0).astype(jnp.bfloat16)

        def back(cols):
            return lax.dot_general(
                d_gate[...], wg[cols, :], contract, preferred_element_type=jnp.float32
            ) + lax.dot_general(
                d_up[...], wu[cols, :], contract, preferred_element_type=jnp.float32
            )

        def outward(cols):
            return jnp.dot(hidden[...], wd[:, cols], preferred_element_type=jnp.float32)

        stores = [
            pltpu.make_async_copy(
                near.at[:, lanes[u]], far_out.at[:, lanes[u]], sems.at[8 + u]
            )
            for u in range(2)
        ]
        put_result(made, rest, back)
        repack(near, 0, scatter, made, rest, extra)
        stores[0].start()
        put_result(made, rest, outward)
        repack(near, LANES, scatter, made, rest)
        stores[1].start()
        for store in stores:
            store.wait()

    return pl.pallas_call(
        kernel,
        out_shape=jax.ShapeDtypeStruct((chunks.shape[0], 2 * LANES), jnp.bfloat16),
        in_specs=[FAR] * 6,
        out_specs=FAR,
        scratch_shapes=[pltpu.VMEM(v.shape, v.dtype) for v in (chunks, *operands)]
        + [
            pltpu.VMEM((640, width), jnp.bfloat16),
            pltpu.VMEM((320, width), jnp.bfloat16),
            pltpu.VMEM((320, units), jnp.bfloat16),
            pltpu.VMEM((320, units), jnp.bfloat16),
            pltpu.VMEM((320, units), jnp.bfloat16),
            pltpu.VMEM((960, LANES), jnp.bfloat16),
            pltpu.VMEM((320, 128), jnp.bfloat16),
            pltpu.VMEM((320, 128), jnp.bfloat16),
            pltpu.SemaphoreType.DMA((10,)),
        ],
        **params(),
    )(chunks, *operands)


def spread_weights(weights, routes):
    tokens = routes[0].shape[0]
    total_rows = 64 * ROWS
    n = len(routes)

    def kernel(*refs):
        w_refs, id_refs, outs = refs[:n], refs[n : 2 * n], refs[2 * n :]
        square = (tokens, tokens)
        before = lax.broadcasted_iota(jnp.int32, square, 1) < lax.broadcasted_iota(
            jnp.int32, square, 0
        )
        shape = (tokens, total_rows)
        expert, row, block, slot = place_of(lax.broadcasted_iota(jnp.int32, shape, 1))
        for at in range(n):
            w, ids = w_refs[at], f32(id_refs[at][...])
            first, second = ids[:, 0:1], ids[:, 1:2]
            first_r, second_r = as_row(first, 1), as_row(second, 1)
            slot_0 = count((first == first_r) & before, 1)
            slot_1 = count(second == first_r, 1) + count((second == second_r) & before, 1)
            key_0, key_1 = first * 8 + slot_0, second * 8 + slot_1

            def spread(key, w=w, key_0=key_0, key_1=key_1):
                key = f32(key)
                total = jnp.where(key_0 == key, w[:, 0:1], 0.0) + jnp.where(
                    key_1 == key, w[:, 1:2], 0.0
                )
                upper = f32(total.astype(jnp.bfloat16))
                return upper, total - upper

            def put(ref, start, values, mask):
                for i, value in enumerate(values):
                    ref[start + tokens * i : start + tokens * i + tokens, :] = jnp.where(
                        mask, value, 0.0
                    ).astype(jnp.bfloat16)

            values = spread(expert * 8 + slot)
            for g in range(3):
                put(outs[2 * at], 2 * tokens * g, values, block == g)
            for s in range(CAP):
                put(outs[2 * at + 1], 2 * tokens * s, spread(expert * 8 + s), row == 15)
            if at == n - 1:
                for k, (chosen, number) in enumerate(((first, slot_0), (second, slot_1))):
                    outs[2 * n][tokens * k : tokens * k + tokens, :] = jnp.where(
                        (row == 15) & (f32(expert) == chosen), 1.0, 0.0
                    ).astype(jnp.bfloat16)
                    outs[2 * n + 1][:, 128 * k : 128 * k + 128] = jnp.broadcast_to(
                        number, (tokens, 128)
                    )

    shapes = [(6 * tokens, total_rows), (2 * CAP * tokens, total_rows)] * n
    shapes.append((2 * tokens, total_rows))
    return pl.pallas_call(
        kernel,
        out_shape=[jax.ShapeDtypeStruct(shape, jnp.bfloat16) for shape in shapes]
        + [jax.ShapeDtypeStruct((tokens, 256), jnp.float32)],
        in_specs=[NEAR] * (2 * n),
        out_specs=[NEAR] * (2 * n + 2),
        **params(),
    )(*weights, *routes)


def finish(chunks, spreads, rows, routes, picked, gain, router_rows):
    forward, saved, cotangent = rows
    tokens, width = forward.shape
    operands = [*spreads, forward, saved, cotangent, routes, picked, gain, router_rows]
    n = len(operands)

    def kernel(far, *refs):
        far_in, out_f, out_b = refs[:n], refs[n], refs[n + 1]
        held = refs[n + 4 : 2 * n + 4]
        result, gradient = refs[n + 2], refs[n + 3]
        near, total, sems = refs[2 * n + 4 :]
        parts_f, tails_f, parts_b, tails_b, picks, slots = held[:6]
        v_f, v_b, cot, ids, chosen, gain_ref, router_ref = held[6:]
        lanes = [pl.ds(u * LANES, LANES) for u in range(2)]
        chunk_loads = [
            pltpu.make_async_copy(far.at[:, lanes[u]], near.at[:, lanes[u]], sems.at[n + u])
            for u in range(2)
        ]
        loads = [
            pltpu.make_async_copy(src, dst, sems.at[i])
            for i, (src, dst) in enumerate(zip(far_in, held))
        ]
        order = [2, 3, 4, 5, 7, 8, 9, 10, 11, 12, 0, 1, 6]
        chunk_loads[0].start()
        for i in order[:10]:
            loads[i].start()
        chunk_loads[1].start()
        for i in order[10:]:
            loads[i].start()

        def add_up(offset, parts, tails, store):
            for c in range(3):
                at = offset + 384 * c
                part = jnp.dot(
                    parts[...], near[:, at : at + 384], preferred_element_type=jnp.float32
                )
                for g in range(3):
                    at = 2 * tokens * g
                    store(
                        g * LANES + 384 * c,
                        384,
                        part[at : at + tokens] + part[at + tokens : at + 2 * tokens],
                    )
            rest = jnp.zeros((2 * tokens, 128), jnp.float32)
            for s in range(CAP):
                rest += jnp.dot(
                    tails[2 * tokens * s : 2 * tokens * (s + 1), :],
                    near[:, offset + 128 * s : offset + 128 * s + 128],
                    preferred_element_type=jnp.float32,
                )
            store(TAIL, 128, rest[:tokens] + rest[tokens:])

        chunk_loads[0].wait()
        for i in order[:10]:
            loads[i].wait()
        found = jnp.dot(picks[...], near[:, 640:768], preferred_element_type=jnp.float32)
        lane = f32(lax.broadcasted_iota(jnp.int32, (tokens, 128), 1))
        inner = [
            jnp.sum(
                jnp.where(
                    lane == slots[:, 128 * k : 128 * k + 128],
                    found[tokens * k : tokens * k + tokens],
                    0.0,
                ),
                axis=1,
                keepdims=True,
            )
            for k in range(2)
        ]
        scores = [chosen[:, k : k + 1] for k in range(2)]
        whole = scores[0] + scores[1]
        mean = (inner[0] * scores[0] + inner[1] * scores[1]) / whole
        numbers = f32(ids[...])
        d_logits = jnp.zeros((tokens, 128), jnp.float32)
        for k in range(2):
            d_logit = (inner[k] - mean) / whole * scores[k] * (1.0 - scores[k])
            d_logits += jnp.where(lane == numbers[:, k : k + 1], d_logit, 0.0)
        pieces, left = [], d_logits
        for _ in range(3):
            pieces.append(left.astype(jnp.bfloat16))
            left = left - f32(pieces[-1])

        def keep(at, size, value):
            for piece in pieces:
                value += jnp.dot(
                    piece, router_ref[:, at : at + size], preferred_element_type=jnp.float32
                )
            total[:, at : at + size] = value

        add_up(0, parts_b, tails_b, keep)
        v = f32(v_b[...])
        inverse = lax.rsqrt(jnp.mean(v * v, axis=-1, keepdims=True) + epsilon)
        scaled = total[...] * gain_ref[...]
        projected = jnp.mean(v * scaled, axis=-1, keepdims=True)
        d_rows = scaled * inverse - v * (inverse * inverse * inverse * projected)
        gradient[...] = (f32(cot[...]) + d_rows).astype(jnp.bfloat16)
        stores = [
            pltpu.make_async_copy(gradient, out_b, sems.at[n + 2]),
            pltpu.make_async_copy(result, out_f, sems.at[n + 3]),
        ]
        stores[0].start()
        chunk_loads[1].wait()
        for i in order[10:]:
            loads[i].wait()

        def put(at, size, value):
            result[:, at : at + size] = (f32(v_f[:, at : at + size]) + value).astype(jnp.bfloat16)

        add_up(LANES, parts_f, tails_f, put)
        stores[1].start()
        for store in stores:
            store.wait()

    row = jax.ShapeDtypeStruct((tokens, width), jnp.bfloat16)
    return pl.pallas_call(
        kernel,
        out_shape=[row, row],
        in_specs=[FAR] * (n + 1),
        out_specs=[FAR] * 2,
        scratch_shapes=[pltpu.VMEM((tokens, width), jnp.bfloat16)] * 2
        + [pltpu.VMEM(v.shape, v.dtype) for v in operands]
        + [
            pltpu.VMEM(chunks.shape, jnp.bfloat16),
            pltpu.VMEM((tokens, width), jnp.float32),
            pltpu.SemaphoreType.DMA((n + 4,)),
        ],
        **params(),
    )(chunks, *operands)


def swapped(chunks):
    shape = chunks.shape
    chunks = chunks.reshape(shape[0] // ROWS, ROWS, shape[1])
    return lax.all_to_all(chunks, "expert", 0, 0, tiled=True).reshape(shape)


def passed_along(x, axis, by):
    n = lax.axis_size(axis)
    return lax.ppermute(x, axis, [(i, (i + by) % n) for i in range(n)])


def normalise(values, gain_row):
    inverse = lax.rsqrt(jnp.mean(values * values, axis=-1, keepdims=True) + epsilon)
    return values * inverse * gain_row


def picked_scores(values, gain_row, router_map, routes):
    normed = normalise(values.astype(jnp.float32), gain_row)
    logits = jnp.dot(normed, router_map.astype(jnp.float32), precision=lax.Precision.HIGHEST)
    scores = jax.nn.sigmoid(logits)
    choices_axis = jnp.arange(router_map.shape[1], dtype=jnp.int32)
    onehot = (routes[:, :, None] == choices_axis[None, None, :]).astype(scores.dtype)
    return jnp.sum(onehot * scores[:, None, :], axis=-1)


def body(
    forward_rows,
    forward_routes,
    saved_rows,
    cotangent,
    backward_routes,
    norm_gain,
    router,
    gate_weight,
    up_weight,
    down_weight,
):
    gain_row, router_map = norm_gain[0], router[0]
    weights = (gate_weight[0, 0], up_weight[0, 0], down_weight[0, 0])
    tables = selections()
    backward_ids, forward_ids = backward_routes[0], forward_routes[0]

    saved, cotan, forward = saved_rows[0], cotangent[0], forward_rows[0]

    sent = pack(
        [(saved, True, 0), (cotan, False, 0), (forward, True, 1)],
        norm_gain,
        [backward_ids, forward_ids],
    )
    received = swapped(sent)
    backward_scores = picked_scores(saved, gain_row, router_map, backward_ids)
    forward_scores = picked_scores(forward, gain_row, router_map, forward_ids)
    spreads = spread_weights(
        [v / jnp.sum(v, axis=1, keepdims=True) for v in (forward_scores, backward_scores)],
        [forward_ids, backward_ids],
    )
    returned = swapped(experts(received, tables, weights))
    router_rows = jnp.pad(router_map.T, ((0, 128 - router_map.shape[1]), (0, 0)))
    result, gradient = finish(
        returned, spreads, (forward, saved, cotan), backward_ids, backward_scores, norm_gain, router_rows
    )
    backward_next = passed_along(gradient[None], "pipe", -1)
    forward_next = passed_along(result[None], "pipe", 1)
    return (forward_next, backward_next)


def solution(mesh):
    in_specs = (
        P("pipe", "expert", None),
        P("pipe", "expert", None),
        P("pipe", "expert", None),
        P("pipe", "expert", None),
        P("pipe", "expert", None),
        P("pipe", None),
        P("pipe", None, None),
        P("pipe", "expert", None, None),
        P("pipe", "expert", None, None),
        P("pipe", "expert", None, None),
    )
    out_specs = (P("pipe", "expert", None), P("pipe", "expert", None))
    return jax.shard_map(body, mesh=mesh, in_specs=in_specs, out_specs=out_specs, check_vma=False)
```

```python
import jax
import jax.numpy as jnp
import numpy as np
from jax import lax
from jax.experimental import pallas as pl
from jax.experimental.pallas import tpu as pltpu
from jax.sharding import PartitionSpec as P

epsilon = 1e-06
VMEM_LIMIT = 60 * 1024 * 1024
CAP = 5
LANES = 1152
ROWS = 16
TAIL = 3 * LANES
FAR = pl.BlockSpec(memory_space=pltpu.HBM)
NEAR = pl.BlockSpec(memory_space=pltpu.VMEM)


def selections():
    gather = np.zeros((256, 256), np.float32)
    for i in range(16):
        gather[240 + i, 16 * i + 15] = 1
        for s in range(CAP):
            for g in range(3):
                gather[80 * g + CAP * i + s, 16 * i + 5 * g + s] = 1
    expand = np.zeros((320, 320), np.float32)
    for i in range(64):
        for s in range(CAP):
            expand[CAP * i + s, 64 * s + i] = 1
    whole = expand.reshape(320, CAP, 64).sum(1)
    chunks = np.concatenate([gather, gather.T])
    slots = np.concatenate([expand, expand.T, whole.T])
    return jnp.asarray(chunks, jnp.bfloat16), jnp.asarray(slots, jnp.bfloat16)


def params():
    return dict(
        compiler_params=pltpu.CompilerParams(vmem_limit_bytes=VMEM_LIMIT),
        cost_estimate=pl.CostEstimate(flops=0, bytes_accessed=1024, transcendentals=0),
    )


def f32(x):
    return x.astype(jnp.float32)


def count(hits, axis):
    return jnp.sum(jnp.where(hits, 1.0, 0.0), axis=axis, keepdims=True)


def place_of(position):
    expert = lax.bitwise_and(lax.shift_right_logical(position, 4), 31)
    row = lax.bitwise_and(position, 15)
    block = jnp.where(row >= 5, 1, 0) + jnp.where(row >= 10, 1, 0) + jnp.where(row >= 15, 1, 0)
    return expert, row, block, row - 5 * block


def as_row(column, copies):
    n = column.shape[0]
    shape = (n, copies * n)
    lane = lax.bitwise_and(lax.broadcasted_iota(jnp.int32, shape, 1), n - 1)
    hit = lax.broadcasted_iota(jnp.int32, shape, 0) == lane
    return jnp.sum(jnp.where(hit, column, 0.0), axis=0, keepdims=True)


def pack(units, gain, routes):
    n, m = len(units), len(routes)
    tokens, width = units[0][0].shape
    half_rows = 32 * ROWS
    operands = [*routes, gain, *[rows for rows, _, _ in units]]

    def kernel(*refs):
        far, out = refs[: n + m + 1], refs[n + m + 1]
        near = refs[n + m + 2 : 2 * (n + m) + 3]
        made, low, high, sems = refs[2 * (n + m) + 3 :]
        loads = [
            pltpu.make_async_copy(src, dst, sems.at[i]) for i, (src, dst) in enumerate(zip(far, near))
        ]
        for load in loads:
            load.start()
        for load in loads[: m + 1]:
            load.wait()
        gain_ref = near[m]
        shape = (half_rows, 2 * tokens)
        expert, row, block, slot = place_of(lax.broadcasted_iota(jnp.int32, shape, 0))
        right = lax.broadcasted_iota(jnp.int32, shape, 1) >= tokens
        stores = []
        for route in range(m):
            ids = f32(near[route][...])
            first, second = ids[:, 0:1], ids[:, 1:2]
            first_r, second_r = as_row(first, 2), as_row(second, 2)
            square = (tokens, 2 * tokens)
            lane = lax.bitwise_and(lax.broadcasted_iota(jnp.int32, square, 1), tokens - 1)
            before = lax.broadcasted_iota(jnp.int32, square, 0) < lane
            slot_0 = count((first == first_r) & before, 0)
            slot_1 = count(first == second_r, 0) + count((second == second_r) & before, 0)
            key_0, key_1 = first_r * 8 + slot_0, second_r * 8 + slot_1

            def hits(key, key_0=key_0, key_1=key_1):
                key = f32(key)
                return (key_0 == key) | (key_1 == key)

            def matrix(mask):
                return jnp.where(mask, 1.0, 0.0).astype(jnp.bfloat16)

            own = hits(expert * 8 + slot)
            pick_low = matrix(own & (block == jnp.where(right, 1, 0)))
            third = own & (block == 2) & ~right
            pick_rest = matrix(third)
            picks = [
                matrix(third | (hits(expert * 8 + s) & (row == 15) & right)) for s in range(CAP)
            ]
            for u in range(n):
                if units[u][2] != route:
                    continue
                loads[m + 1 + u].wait()
                x = near[m + 1 + u][...]
                if units[u][1]:
                    v = f32(x)
                    inverse = lax.rsqrt(jnp.mean(v * v, axis=-1, keepdims=True) + epsilon)
                    x = (v * inverse * gain_ref[...]).astype(jnp.bfloat16)
                low[0:tokens, :] = x[:, :LANES]
                low[tokens:, :] = x[:, LANES : 2 * LANES]
                high[0:tokens, :] = x[:, 2 * LANES : TAIL]
                high[tokens:, :] = jnp.zeros((tokens, LANES), jnp.bfloat16)
                for s in range(CAP):
                    high[tokens:, 128 * s : 128 * s + 128] = x[:, TAIL:]
                for s in range(9):
                    cols = slice(128 * s, 128 * s + 128)
                    part = jnp.dot(pick_low, low[:, cols], preferred_element_type=jnp.float32)
                    part += jnp.dot(
                        picks[s] if s < CAP else pick_rest,
                        high[:, cols],
                        preferred_element_type=jnp.float32,
                    )
                    made[:, u * LANES + 128 * s : u * LANES + 128 * s + 128] = part.astype(
                        jnp.bfloat16
                    )
                lanes = pl.ds(u * LANES, LANES)
                for r in range(2):
                    stores.append(
                        pltpu.make_async_copy(
                            made.at[:, lanes],
                            out.at[pl.ds(half_rows * r, half_rows), lanes],
                            sems.at[n + m + 1 + 2 * u + r],
                        )
                    )
                    stores[-1].start()
        for store in stores:
            store.wait()

    return pl.pallas_call(
        kernel,
        out_shape=jax.ShapeDtypeStruct((2 * half_rows, n * LANES), jnp.bfloat16),
        in_specs=[FAR] * (n + m + 1),
        out_specs=FAR,
        scratch_shapes=[pltpu.VMEM(v.shape, v.dtype) for v in operands]
        + [
            pltpu.VMEM((half_rows, n * LANES), jnp.bfloat16),
            pltpu.VMEM((2 * tokens, LANES), jnp.bfloat16),
            pltpu.VMEM((2 * tokens, LANES), jnp.bfloat16),
            pltpu.SemaphoreType.DMA((3 * n + m + 1,)),
        ],
        **params(),
    )(*operands)


def unpack(chunks, offset, tables, x, start, last, stacked):
    gather, expand = tables

    for b in range(4):
        held = slice(256 * b, 256 * b + 256)
        rows = slice(start + 80 * b, start + 80 * b + 80)
        for c in range(3):
            part = jnp.dot(
                gather[:256, :],
                chunks[held, offset + 384 * c : offset + 384 * c + 384],
                preferred_element_type=jnp.float32,
            ).astype(jnp.bfloat16)
            for g in range(3):
                at = g * LANES + 384 * c
                x[rows, at : at + 384] = part[80 * g : 80 * g + 80]
            last[16 * b : 16 * b + 16, 384 * c : 384 * c + 384] = part[240:]
    for s in range(CAP):
        stacked[64 * s : 64 * s + 64, :] = last[:, 128 * s : 128 * s + 128]
    x[start : start + 320, TAIL:] = jnp.dot(
        expand[:320, :], stacked[...], preferred_element_type=jnp.float32
    ).astype(jnp.bfloat16)


def repack(chunks, offset, tables, made, rest, extra=None):
    gather, expand = tables
    tail = jnp.dot(
        expand[320:640, :], rest[...], preferred_element_type=jnp.float32
    ).astype(jnp.bfloat16)
    spare = jnp.zeros((64, 128), jnp.bfloat16)
    if extra is not None:
        spare = jnp.dot(
            expand[640:, :], extra[...], preferred_element_type=jnp.float32
        ).astype(jnp.bfloat16)
    for b in range(4):
        at = slice(256 * b + 240, 256 * b + 256)
        for s in range(CAP):
            made[at, 128 * s : 128 * s + 128] = tail[64 * s + 16 * b : 64 * s + 16 * b + 16]
        made[at, 640:768] = spare[16 * b : 16 * b + 16]
        made[at, 768:] = jnp.zeros((16, LANES - 768), jnp.bfloat16)

    for b in range(4):
        held = slice(256 * b, 256 * b + 256)
        chunks[held, offset : offset + LANES] = jnp.dot(
            gather[256:, :], made[held, :], preferred_element_type=jnp.float32
        ).astype(jnp.bfloat16)


def put_result(made, rest, product):
    for g in range(3):
        part = product(pl.ds(g * LANES, LANES)).astype(jnp.bfloat16)
        for b in range(4):
            made[256 * b + 80 * g : 256 * b + 80 * g + 80, :] = part[80 * b : 80 * b + 80]
    rest[...] = product(pl.ds(TAIL, 128)).astype(jnp.bfloat16)


def load_all(far, near, sems, first=0):
    return [
        pltpu.make_async_copy(src, dst, sems.at[first + n])
        for n, (src, dst) in enumerate(zip(far, near))
    ]


def experts_forward(chunks, offset, tables, weights):
    width, units = weights[0].shape
    half = units // 2

    def kernel(far, *refs):
        far_in, far_out = refs[:5], refs[5]
        near, gather, expand, wg, wu, wd, x, hidden, made, rest, last, stacked, sems = refs[6:]
        tables = (gather, expand)
        part = pltpu.make_async_copy(far.at[:, pl.ds(offset, LANES)], near, sems.at[0])
        loads = load_all(
            (far_in[0], far_in[1], far_in[4]), (gather, expand, wd), sems, 1
        )
        pieces = []
        for k in range(2):
            cols = pl.ds(half * k, half)
            pieces += load_all(
                (far_in[2].at[:, cols], far_in[3].at[:, cols]),
                (wg.at[:, cols], wu.at[:, cols]),
                sems,
                4 + 2 * k,
            )
        for load in (part, loads[0], loads[1], *pieces, loads[2]):
            load.start()
        part.wait()
        loads[0].wait()
        loads[1].wait()
        unpack(near, 0, tables, x, 0, last, stacked)
        for k in range(2):
            pieces[2 * k].wait()
            pieces[2 * k + 1].wait()
            cols = pl.ds(half * k, half)
            gate = jnp.dot(x[...], wg[:, cols], preferred_element_type=jnp.float32)
            upper = jnp.dot(x[...], wu[:, cols], preferred_element_type=jnp.float32)
            hidden[:, cols] = (gate * jax.nn.sigmoid(gate) * upper).astype(jnp.bfloat16)
        loads[2].wait()
        put_result(
            made,
            rest,
            lambda cols: jnp.dot(hidden[...], wd[:, cols], preferred_element_type=jnp.float32),
        )
        repack(near, 0, tables, made, rest)
        store = pltpu.make_async_copy(near, far_out, sems.at[8])
        store.start()
        store.wait()

    rows = chunks.shape[0]
    return pl.pallas_call(
        kernel,
        out_shape=jax.ShapeDtypeStruct((rows, LANES), jnp.bfloat16),
        in_specs=[FAR] * 6,
        out_specs=FAR,
        scratch_shapes=[pltpu.VMEM((rows, LANES), jnp.bfloat16)]
        + [pltpu.VMEM(v.shape, v.dtype) for v in (*tables, *weights)]
        + [
            pltpu.VMEM((320, width), jnp.bfloat16),
            pltpu.VMEM((320, units), jnp.bfloat16),
            pltpu.VMEM((1024, LANES), jnp.bfloat16),
            pltpu.VMEM((320, 128), jnp.bfloat16),
            pltpu.VMEM((64, LANES), jnp.bfloat16),
            pltpu.VMEM((320, 128), jnp.bfloat16),
            pltpu.SemaphoreType.DMA((9,)),
        ],
        **params(),
    )(chunks, *tables, *weights)


def experts_backward(chunks, tables, weights, after):
    width, units = weights[0].shape
    contract = (((1,), (1,)), ((), ()))

    def kernel(far, *refs):
        far_in, far_out = refs[:5], refs[6]
        near, gather, expand, wg, wu, wd = refs[7:13]
        x, cot, d_gate, d_up, made, rest, extra, last, stacked, sems = refs[13:]
        tables = (gather, expand)
        parts = load_all(
            [far.at[:, pl.ds(u * LANES, LANES)] for u in range(2)],
            [near.at[:, pl.ds(u * LANES, LANES)] for u in range(2)],
            sems,
        )
        loads = load_all(far_in, (gather, expand, wg, wu, wd), sems, 2)
        for load in (parts[0], loads[0], loads[1], parts[1], *loads[2:]):
            load.start()
        parts[0].wait()
        loads[0].wait()
        loads[1].wait()
        unpack(near, 0, tables, x, 0, last, stacked)
        parts[1].wait()
        unpack(near, LANES, tables, cot, 0, last, stacked)
        for load in loads[2:]:
            load.wait()

        def step(k, inner):
            cols = pl.ds(pl.multiple_of(k * 256, 256), 256)
            gate = jnp.dot(x[...], wg[:, cols], preferred_element_type=jnp.float32)
            upper = jnp.dot(x[...], wu[:, cols], preferred_element_type=jnp.float32)
            d_hidden = lax.dot_general(
                cot[...], wd[cols, :], contract, preferred_element_type=jnp.float32
            )
            s = jax.nn.sigmoid(gate)
            active = gate * s
            value = f32((active * upper).astype(jnp.bfloat16))
            d_gate[:, cols] = (d_hidden * upper * s * (1.0 + gate * (1.0 - s))).astype(
                jnp.bfloat16
            )
            d_up[:, cols] = (d_hidden * active).astype(jnp.bfloat16)
            return inner + jnp.sum(value * d_hidden, axis=1, keepdims=True)

        inner = lax.fori_loop(0, units // 256, step, jnp.zeros((320, 1), jnp.float32))
        slot = lax.rem(lax.broadcasted_iota(jnp.int32, (320, 128), 0), CAP)
        lane = lax.broadcasted_iota(jnp.int32, (320, 128), 1)
        extra[...] = jnp.where(slot == lane, inner, 0.0).astype(jnp.bfloat16)

        def back(cols):
            return lax.dot_general(
                d_gate[...], wg[cols, :], contract, preferred_element_type=jnp.float32
            ) + lax.dot_general(
                d_up[...], wu[cols, :], contract, preferred_element_type=jnp.float32
            )

        put_result(made, rest, back)
        repack(near, 0, tables, made, rest, extra)
        store = pltpu.make_async_copy(near.at[:, pl.ds(0, LANES)], far_out, sems.at[7])
        store.start()
        store.wait()

    rows = chunks.shape[0]
    return pl.pallas_call(
        kernel,
        out_shape=jax.ShapeDtypeStruct((rows, LANES), jnp.bfloat16),
        in_specs=[FAR] * 6 + [pl.BlockSpec(memory_space=pl.ANY)],
        out_specs=FAR,
        scratch_shapes=[pltpu.VMEM((rows, 2 * LANES), jnp.bfloat16)]
        + [pltpu.VMEM(v.shape, v.dtype) for v in (*tables, *weights)]
        + [
            pltpu.VMEM((320, width), jnp.bfloat16),
            pltpu.VMEM((320, width), jnp.bfloat16),
            pltpu.VMEM((320, units), jnp.bfloat16),
            pltpu.VMEM((320, units), jnp.bfloat16),
            pltpu.VMEM((1024, LANES), jnp.bfloat16),
            pltpu.VMEM((320, 128), jnp.bfloat16),
            pltpu.VMEM((320, 128), jnp.bfloat16),
            pltpu.VMEM((64, LANES), jnp.bfloat16),
            pltpu.VMEM((320, 128), jnp.bfloat16),
            pltpu.SemaphoreType.DMA((8,)),
        ],
        **params(),
    )(chunks, *tables, *weights, after)


def spread_weights(weights, routes):
    tokens = routes[0].shape[0]
    total_rows = 64 * ROWS
    n = len(routes)

    def kernel(*refs):
        w_refs, id_refs, outs = refs[:n], refs[n : 2 * n], refs[2 * n :]
        square = (tokens, tokens)
        before = lax.broadcasted_iota(jnp.int32, square, 1) < lax.broadcasted_iota(
            jnp.int32, square, 0
        )
        shape = (tokens, total_rows)
        expert, row, block, slot = place_of(lax.broadcasted_iota(jnp.int32, shape, 1))
        place = lax.broadcasted_iota(jnp.int32, (tokens, 64 * CAP), 1)
        place = lax.bitwise_and(place, 31) * 8 + lax.shift_right_logical(place, 6)
        for at in range(n):
            w, ids = w_refs[at], f32(id_refs[at][...])
            first, second = ids[:, 0:1], ids[:, 1:2]
            first_r, second_r = as_row(first, 1), as_row(second, 1)
            slot_0 = count((first == first_r) & before, 1)
            slot_1 = count(second == first_r, 1) + count((second == second_r) & before, 1)
            key_0, key_1 = first * 8 + slot_0, second * 8 + slot_1

            def spread(key, w=w, key_0=key_0, key_1=key_1):
                key = f32(key)
                total = jnp.where(key_0 == key, w[:, 0:1], 0.0) + jnp.where(
                    key_1 == key, w[:, 1:2], 0.0
                )
                upper = f32(total.astype(jnp.bfloat16))
                return upper, total - upper

            for i, value in enumerate(spread(expert * 8 + slot)):
                for g in range(3):
                    start = 2 * tokens * g + tokens * i
                    outs[2 * at][start : start + tokens, :] = jnp.where(
                        block == g, value, 0.0
                    ).astype(jnp.bfloat16)
            for i, value in enumerate(spread(place)):
                outs[2 * at + 1][tokens * i : tokens * i + tokens, :] = value.astype(jnp.bfloat16)
            if at == n - 1:
                source = lax.broadcasted_iota(jnp.int32, (tokens, 64), 1)
                source = f32(lax.bitwise_and(source, 31))
                for k, (chosen, number) in enumerate(((first, slot_0), (second, slot_1))):
                    outs[2 * n][tokens * k : tokens * k + tokens, :] = jnp.where(
                        source == chosen, 1.0, 0.0
                    ).astype(jnp.bfloat16)
                    outs[2 * n + 1][:, 128 * k : 128 * k + 128] = jnp.broadcast_to(
                        number, (tokens, 128)
                    )

    shapes = [(6 * tokens, total_rows), (2 * tokens, 64 * CAP)] * n + [(2 * tokens, 64)]
    return pl.pallas_call(
        kernel,
        out_shape=[jax.ShapeDtypeStruct(shape, jnp.bfloat16) for shape in shapes]
        + [jax.ShapeDtypeStruct((tokens, 256), jnp.float32)],
        in_specs=[NEAR] * (2 * n),
        out_specs=[NEAR] * (2 * n + 2),
        **params(),
    )(*weights, *routes)


def last_rows(near, columns):
    shape = (64, 64 * ROWS)
    wanted = lax.broadcasted_iota(jnp.int32, shape, 0) * ROWS + (ROWS - 1)
    pick = jnp.where(wanted == lax.broadcasted_iota(jnp.int32, shape, 1), 1.0, 0.0)
    return jnp.dot(
        pick.astype(jnp.bfloat16), near[:, :columns], preferred_element_type=jnp.float32
    ).astype(jnp.bfloat16)


def add_up(near, rows_15, stacked, parts, tails, store):
    tokens = tails.shape[0] // 2
    for s in range(CAP):
        stacked[64 * s : 64 * s + 64, :] = rows_15[:, 128 * s : 128 * s + 128]
    rest = jnp.dot(tails[...], stacked[...], preferred_element_type=jnp.float32)
    store(TAIL, 128, rest[:tokens] + rest[tokens:])
    for c in range(3):
        part = jnp.dot(
            parts[...], near[:, 384 * c : 384 * c + 384], preferred_element_type=jnp.float32
        )
        for g in range(3):
            at = 2 * tokens * g
            store(
                g * LANES + 384 * c,
                384,
                part[at : at + tokens] + part[at + tokens : at + 2 * tokens],
            )


def finish_forward(chunks, parts, tails, rows):
    tokens, width = rows.shape
    operands = [chunks, parts, tails, rows]

    def kernel(*refs):
        out, held, result, stacked, sems = refs[4], refs[5:9], refs[9], refs[10], refs[11]
        near, parts, tails, v = held
        loads = load_all(refs[:4], held, sems)
        for load in loads:
            load.start()
        for load in loads:
            load.wait()

        def put(at, size, value):
            result[:, at : at + size] = (f32(v[:, at : at + size]) + value).astype(jnp.bfloat16)

        add_up(near, last_rows(near, 640), stacked, parts, tails, put)
        store = pltpu.make_async_copy(result, out, sems.at[4])
        store.start()
        store.wait()

    return pl.pallas_call(
        kernel,
        out_shape=jax.ShapeDtypeStruct((tokens, width), jnp.bfloat16),
        in_specs=[FAR] * 4,
        out_specs=FAR,
        scratch_shapes=[pltpu.VMEM(v.shape, v.dtype) for v in operands]
        + [
            pltpu.VMEM((tokens, width), jnp.bfloat16),
            pltpu.VMEM((64 * CAP, 128), jnp.bfloat16),
            pltpu.SemaphoreType.DMA((5,)),
        ],
        **params(),
    )(*operands)


def finish_backward(chunks, spreads, rows, cotangent, routes, picked, gain, router_rows):
    tokens, width = rows.shape
    operands = [chunks, *spreads, rows, cotangent, routes, picked, gain, router_rows]
    n = len(operands)

    def kernel(*refs):
        out, held = refs[n], refs[n + 1 : 2 * n + 1]
        gradient, total, stacked, sems = refs[2 * n + 1 :]
        near, parts, tails, picks, slots, v_ref, cot, ids, chosen, gain_ref, router_ref = held
        loads = load_all(refs[:n], held, sems)
        for load in loads:
            load.start()
        for load in loads:
            load.wait()
        rows_15 = last_rows(near, 768)
        found = jnp.dot(picks[...], rows_15[:, 640:], preferred_element_type=jnp.float32)
        lane = f32(lax.broadcasted_iota(jnp.int32, (tokens, 128), 1))
        inner = [
            jnp.sum(
                jnp.where(
                    lane == slots[:, 128 * k : 128 * k + 128],
                    found[tokens * k : tokens * k + tokens],
                    0.0,
                ),
                axis=1,
                keepdims=True,
            )
            for k in range(2)
        ]
        scores = [chosen[:, k : k + 1] for k in range(2)]
        whole = scores[0] + scores[1]
        mean = (inner[0] * scores[0] + inner[1] * scores[1]) / whole
        numbers = f32(ids[...])
        d_logits = jnp.zeros((tokens, 128), jnp.float32)
        for k in range(2):
            d_logit = (inner[k] - mean) / whole * scores[k] * (1.0 - scores[k])
            d_logits += jnp.where(lane == numbers[:, k : k + 1], d_logit, 0.0)
        pieces, left = [], d_logits
        for _ in range(3):
            pieces.append(left.astype(jnp.bfloat16))
            left = left - f32(pieces[-1])
        pieces = jnp.concatenate(pieces, axis=0)

        def keep(at, size, value):
            routed = jnp.dot(
                pieces, router_ref[:, at : at + size], preferred_element_type=jnp.float32
            )
            for i in range(3):
                value += routed[tokens * i : tokens * i + tokens]
            total[:, at : at + size] = value * gain_ref[:, at : at + size]

        add_up(near, rows_15, stacked, parts, tails, keep)
        v = f32(v_ref[...])
        inverse = lax.rsqrt(jnp.mean(v * v, axis=-1, keepdims=True) + epsilon)
        projected = jnp.mean(v * total[...], axis=-1, keepdims=True)
        d_rows = total[...] * inverse - v * (inverse * inverse * inverse * projected)
        gradient[...] = (f32(cot[...]) + d_rows).astype(jnp.bfloat16)
        store = pltpu.make_async_copy(gradient, out, sems.at[n])
        store.start()
        store.wait()

    return pl.pallas_call(
        kernel,
        out_shape=jax.ShapeDtypeStruct((tokens, width), jnp.bfloat16),
        in_specs=[FAR] * n,
        out_specs=FAR,
        scratch_shapes=[pltpu.VMEM(v.shape, v.dtype) for v in operands]
        + [
            pltpu.VMEM((tokens, width), jnp.bfloat16),
            pltpu.VMEM((tokens, width), jnp.float32),
            pltpu.VMEM((64 * CAP, 128), jnp.bfloat16),
            pltpu.SemaphoreType.DMA((n + 1,)),
        ],
        **params(),
    )(*operands)


def swapped(chunks):
    shape = chunks.shape
    chunks = chunks.reshape(shape[0] // ROWS, ROWS, shape[1])
    return lax.all_to_all(chunks, "expert", 0, 0, tiled=True).reshape(shape)


def passed_along(x, axis, by):
    n = lax.axis_size(axis)
    return lax.ppermute(x, axis, [(i, (i + by) % n) for i in range(n)])


def normalise(values, gain_row):
    inverse = lax.rsqrt(jnp.mean(values * values, axis=-1, keepdims=True) + epsilon)
    return values * inverse * gain_row


def picked_scores(values, gain_row, router_map, routes):
    normed = normalise(values.astype(jnp.float32), gain_row)
    logits = jnp.dot(normed, router_map.astype(jnp.float32), precision=lax.Precision.HIGHEST)
    scores = jax.nn.sigmoid(logits)
    choices_axis = jnp.arange(router_map.shape[1], dtype=jnp.int32)
    onehot = (routes[:, :, None] == choices_axis[None, None, :]).astype(scores.dtype)
    return jnp.sum(onehot * scores[:, None, :], axis=-1)


def body(
    forward_rows,
    forward_routes,
    saved_rows,
    cotangent,
    backward_routes,
    norm_gain,
    router,
    gate_weight,
    up_weight,
    down_weight,
):
    gain_row, router_map = norm_gain[0], router[0]
    weights = (gate_weight[0, 0], up_weight[0, 0], down_weight[0, 0])
    tables = selections()
    backward_ids, forward_ids = backward_routes[0], forward_routes[0]

    saved, cotan, forward = saved_rows[0], cotangent[0], forward_rows[0]

    sent = pack(
        [(saved, True, 0), (cotan, False, 0), (forward, True, 1)],
        norm_gain,
        [backward_ids, forward_ids],
    )
    received = swapped(sent)
    backward_scores = picked_scores(saved, gain_row, router_map, backward_ids)
    forward_scores = picked_scores(forward, gain_row, router_map, forward_ids)
    spreads = spread_weights(
        [v / jnp.sum(v, axis=1, keepdims=True) for v in (forward_scores, backward_scores)],
        [forward_ids, backward_ids],
    )
    forward_chunks = experts_forward(received, 2 * LANES, tables, weights)
    backward_chunks = experts_backward(received, tables, weights, forward_chunks)
    forward_back, backward_back = swapped(forward_chunks), swapped(backward_chunks)
    router_rows = jnp.pad(router_map.T, ((0, 128 - router_map.shape[1]), (0, 0)))
    result = finish_forward(forward_back, spreads[0], spreads[1], forward)
    gradient = finish_backward(
        backward_back,
        spreads[2:],
        saved,
        cotan,
        backward_ids,
        backward_scores,
        norm_gain,
        router_rows,
    )
    backward_next = passed_along(gradient[None], "pipe", -1)
    forward_next = passed_along(result[None], "pipe", 1)
    return (forward_next, backward_next)


def solution(mesh):
    in_specs = (
        P("pipe", "expert", None),
        P("pipe", "expert", None),
        P("pipe", "expert", None),
        P("pipe", "expert", None),
        P("pipe", "expert", None),
        P("pipe", None),
        P("pipe", None, None),
        P("pipe", "expert", None, None),
        P("pipe", "expert", None, None),
        P("pipe", "expert", None, None),
    )
    out_specs = (P("pipe", "expert", None), P("pipe", "expert", None))
    return jax.shard_map(body, mesh=mesh, in_specs=in_specs, out_specs=out_specs, check_vma=False)
```

```python
import jax
import jax.numpy as jnp
import numpy as np
from jax import lax
from jax.experimental import pallas as pl
from jax.experimental.pallas import tpu as pltpu
from jax.sharding import PartitionSpec as P

epsilon = 1e-06
VMEM_LIMIT = 60 * 1024 * 1024
CAP = 5
LANES = 1152
ROWS = 16
TAIL = 3 * LANES
FAR = pl.BlockSpec(memory_space=pltpu.HBM)
NEAR = pl.BlockSpec(memory_space=pltpu.VMEM)


def selections():
    gather = np.zeros((256, 256), np.float32)
    for i in range(16):
        gather[240 + i, 16 * i + 15] = 1
        for s in range(CAP):
            for g in range(3):
                gather[80 * g + CAP * i + s, 16 * i + 5 * g + s] = 1
    expand = np.zeros((320, 320), np.float32)
    for i in range(64):
        for s in range(CAP):
            expand[CAP * i + s, 64 * s + i] = 1
    whole = expand.reshape(320, CAP, 64).sum(1)
    chunks = np.concatenate([gather, gather.T])
    slots = np.concatenate([expand, expand.T, whole.T])
    return jnp.asarray(chunks, jnp.bfloat16), jnp.asarray(slots, jnp.bfloat16)


def params():
    return dict(
        compiler_params=pltpu.CompilerParams(vmem_limit_bytes=VMEM_LIMIT),
        cost_estimate=pl.CostEstimate(flops=0, bytes_accessed=1024, transcendentals=0),
    )


def f32(x):
    return x.astype(jnp.float32)


def count(hits, axis):
    return jnp.sum(jnp.where(hits, 1.0, 0.0), axis=axis, keepdims=True)


def place_of(position):
    expert = lax.bitwise_and(lax.shift_right_logical(position, 4), 31)
    row = lax.bitwise_and(position, 15)
    block = jnp.where(row >= 5, 1, 0) + jnp.where(row >= 10, 1, 0) + jnp.where(row >= 15, 1, 0)
    return expert, row, block, row - 5 * block


def as_row(column, copies):
    n = column.shape[0]
    shape = (n, copies * n)
    lane = lax.bitwise_and(lax.broadcasted_iota(jnp.int32, shape, 1), n - 1)
    hit = lax.broadcasted_iota(jnp.int32, shape, 0) == lane
    return jnp.sum(jnp.where(hit, column, 0.0), axis=0, keepdims=True)


def as_column(row):
    shape = (row.shape[1], row.shape[1])
    hit = lax.broadcasted_iota(jnp.int32, shape, 0) == lax.broadcasted_iota(jnp.int32, shape, 1)
    return jnp.sum(jnp.where(hit, row, 0.0), axis=1, keepdims=True)


def pack(units, gain, routes):
    n, m = len(units), len(routes)
    tokens, width = units[0][0].shape
    half_rows = 32 * ROWS
    operands = [*routes, gain, *[rows for rows, _, _ in units]]

    def kernel(*refs):
        far, out = refs[: n + m + 1], refs[n + m + 1]
        near = refs[n + m + 2 : 2 * (n + m) + 3]
        made, stacked, sems = refs[2 * (n + m) + 3 :]
        loads = [
            pltpu.make_async_copy(src, dst, sems.at[i]) for i, (src, dst) in enumerate(zip(far, near))
        ]
        for load in loads:
            load.start()
        for load in loads[: m + 1]:
            load.wait()
        gain_ref = near[m]
        shape = (half_rows, 4 * tokens)
        expert, row, block, slot = place_of(lax.broadcasted_iota(jnp.int32, shape, 0))
        lane = lax.broadcasted_iota(jnp.int32, shape, 1)
        body_lanes = (lane < 3 * tokens) & (block == lax.shift_right_logical(lane, 6))
        tail_lanes = (row == 15) & (lane == 3 * tokens + expert)
        place = lax.broadcasted_iota(jnp.int32, (32 * CAP, tokens), 0)
        tail_key = lax.bitwise_and(place, 31) * 8 + lax.shift_right_logical(place, 5)
        stores = []
        stacked[3 * tokens :, :] = jnp.zeros((tokens, LANES), jnp.bfloat16)
        for route in range(m):
            ids = f32(near[route][...])
            first, second = as_column(ids[0:1, :]), as_column(ids[1:2, :])
            first_r, second_r = as_row(first, 4), as_row(second, 4)
            square = (tokens, 4 * tokens)
            other = lax.bitwise_and(lax.broadcasted_iota(jnp.int32, square, 1), tokens - 1)
            before = lax.broadcasted_iota(jnp.int32, square, 0) < other
            slot_0 = count((first == first_r) & before, 0)
            slot_1 = count(first == second_r, 0) + count((second == second_r) & before, 0)
            key_0, key_1 = first_r * 8 + slot_0, second_r * 8 + slot_1
            key = f32(expert * 8 + slot)
            own = ((key_0 == key) | (key_1 == key)) & body_lanes
            pick = jnp.where(own | tail_lanes, 1.0, 0.0).astype(jnp.bfloat16)
            key = f32(tail_key)
            hit = (key_0[:, :tokens] == key) | (key_1[:, :tokens] == key)
            pick_tail = jnp.where(hit, 1.0, 0.0).astype(jnp.bfloat16)
            for u in range(n):
                if units[u][2] != route:
                    continue
                loads[m + 1 + u].wait()
                x = near[m + 1 + u][...]
                if units[u][1]:
                    v = f32(x)
                    inverse = lax.rsqrt(jnp.mean(v * v, axis=-1, keepdims=True) + epsilon)
                    x = (v * inverse * gain_ref[...]).astype(jnp.bfloat16)
                for g in range(3):
                    stacked[tokens * g : tokens * g + tokens, :] = x[:, g * LANES : (g + 1) * LANES]
                tail = jnp.dot(
                    pick_tail, x[:, TAIL:], preferred_element_type=jnp.float32
                ).astype(jnp.bfloat16)
                for s in range(CAP):
                    stacked[3 * tokens : 3 * tokens + 32, 128 * s : 128 * s + 128] = tail[
                        32 * s : 32 * s + 32
                    ]
                for c in range(3):
                    at = u * LANES + 384 * c
                    made[:, at : at + 384] = jnp.dot(
                        pick,
                        stacked[:, 384 * c : 384 * c + 384],
                        preferred_element_type=jnp.float32,
                    ).astype(jnp.bfloat16)
                lanes = pl.ds(u * LANES, LANES)
                for r in range(2):
                    stores.append(
                        pltpu.make_async_copy(
                            made.at[:, lanes],
                            out.at[pl.ds(half_rows * r, half_rows), lanes],
                            sems.at[n + m + 1 + 2 * u + r],
                        )
                    )
                    stores[-1].start()
        for store in stores:
            store.wait()

    return pl.pallas_call(
        kernel,
        out_shape=jax.ShapeDtypeStruct((2 * half_rows, n * LANES), jnp.bfloat16),
        in_specs=[FAR] * (n + m + 1),
        out_specs=FAR,
        scratch_shapes=[pltpu.VMEM(v.shape, v.dtype) for v in operands]
        + [
            pltpu.VMEM((half_rows, n * LANES), jnp.bfloat16),
            pltpu.VMEM((4 * tokens, LANES), jnp.bfloat16),
            pltpu.SemaphoreType.DMA((3 * n + m + 1,)),
        ],
        **params(),
    )(*operands)


def unpack(chunks, offset, tables, x, start, last, stacked):
    gather, expand = tables

    for b in range(4):
        held = slice(256 * b, 256 * b + 256)
        rows = slice(start + 80 * b, start + 80 * b + 80)
        for c in range(3):
            part = jnp.dot(
                gather[:256, :],
                chunks[held, offset + 384 * c : offset + 384 * c + 384],
                preferred_element_type=jnp.float32,
            ).astype(jnp.bfloat16)
            for g in range(3):
                at = g * LANES + 384 * c
                x[rows, at : at + 384] = part[80 * g : 80 * g + 80]
            last[16 * b : 16 * b + 16, 384 * c : 384 * c + 384] = part[240:]
    for s in range(CAP):
        stacked[64 * s : 64 * s + 64, :] = last[:, 128 * s : 128 * s + 128]
    x[start : start + 320, TAIL:] = jnp.dot(
        expand[:320, :], stacked[...], preferred_element_type=jnp.float32
    ).astype(jnp.bfloat16)


def repack(chunks, offset, tables, made, rest, extra=None, stores=()):
    gather, expand = tables
    tail = jnp.dot(
        expand[320:640, :], rest[...], preferred_element_type=jnp.float32
    ).astype(jnp.bfloat16)
    spare = jnp.zeros((64, 128), jnp.bfloat16)
    if extra is not None:
        spare = jnp.dot(
            expand[640:, :], extra[...], preferred_element_type=jnp.float32
        ).astype(jnp.bfloat16)
    for b in range(4):
        at = slice(256 * b + 240, 256 * b + 256)
        for s in range(CAP):
            made[at, 128 * s : 128 * s + 128] = tail[64 * s + 16 * b : 64 * s + 16 * b + 16]
        made[at, 640:768] = spare[16 * b : 16 * b + 16]
        made[at, 768:] = jnp.zeros((16, LANES - 768), jnp.bfloat16)

    for b in range(4):
        held = slice(256 * b, 256 * b + 256)
        chunks[held, offset : offset + LANES] = jnp.dot(
            gather[256:, :], made[held, :], preferred_element_type=jnp.float32
        ).astype(jnp.bfloat16)
        if stores:
            stores[b].start()
    for store in stores:
        store.wait()


def put_result(made, rest, product):
    for g in range(3):
        part = product(pl.ds(g * LANES, LANES)).astype(jnp.bfloat16)
        for b in range(4):
            made[256 * b + 80 * g : 256 * b + 80 * g + 80, :] = part[80 * b : 80 * b + 80]
    rest[...] = product(pl.ds(TAIL, 128)).astype(jnp.bfloat16)


def load_all(far, near, sems, first=0):
    return [
        pltpu.make_async_copy(src, dst, sems.at[first + n])
        for n, (src, dst) in enumerate(zip(far, near))
    ]


def experts_forward(chunks, offset, tables, weights):
    width, units = weights[0].shape
    half = units // 2

    def kernel(far, *refs):
        far_in, far_out = refs[:5], refs[5]
        near, gather, expand, wg, wu, wd, x, hidden, made, rest, last, stacked, sems = refs[6:]
        tables = (gather, expand)
        part = pltpu.make_async_copy(far.at[:, pl.ds(offset, LANES)], near, sems.at[0])
        loads = load_all(
            (far_in[0], far_in[1], far_in[4]), (gather, expand, wd), sems, 1
        )
        pieces = []
        for k in range(2):
            cols = pl.ds(half * k, half)
            pieces += load_all(
                (far_in[2].at[:, cols], far_in[3].at[:, cols]),
                (wg.at[:, cols], wu.at[:, cols]),
                sems,
                4 + 2 * k,
            )
        for load in (part, loads[0], loads[1], *pieces, loads[2]):
            load.start()
        part.wait()
        loads[0].wait()
        loads[1].wait()
        unpack(near, 0, tables, x, 0, last, stacked)
        for k in range(2):
            pieces[2 * k].wait()
            pieces[2 * k + 1].wait()
            cols = pl.ds(half * k, half)
            gate = jnp.dot(x[...], wg[:, cols], preferred_element_type=jnp.float32)
            upper = jnp.dot(x[...], wu[:, cols], preferred_element_type=jnp.float32)
            hidden[:, cols] = (gate * jax.nn.sigmoid(gate) * upper).astype(jnp.bfloat16)
        loads[2].wait()
        put_result(
            made,
            rest,
            lambda cols: jnp.dot(hidden[...], wd[:, cols], preferred_element_type=jnp.float32),
        )
        stores = [
            pltpu.make_async_copy(
                near.at[pl.ds(256 * b, 256)], far_out.at[pl.ds(256 * b, 256)], sems.at[8 + b]
            )
            for b in range(4)
        ]
        repack(near, 0, tables, made, rest, stores=stores)

    rows = chunks.shape[0]
    return pl.pallas_call(
        kernel,
        out_shape=jax.ShapeDtypeStruct((rows, LANES), jnp.bfloat16),
        in_specs=[FAR] * 6,
        out_specs=FAR,
        scratch_shapes=[pltpu.VMEM((rows, LANES), jnp.bfloat16)]
        + [pltpu.VMEM(v.shape, v.dtype) for v in (*tables, *weights)]
        + [
            pltpu.VMEM((320, width), jnp.bfloat16),
            pltpu.VMEM((320, units), jnp.bfloat16),
            pltpu.VMEM((1024, LANES), jnp.bfloat16),
            pltpu.VMEM((320, 128), jnp.bfloat16),
            pltpu.VMEM((64, LANES), jnp.bfloat16),
            pltpu.VMEM((320, 128), jnp.bfloat16),
            pltpu.SemaphoreType.DMA((12,)),
        ],
        **params(),
    )(chunks, *tables, *weights)


def experts_backward(chunks, tables, weights, after):
    width, units = weights[0].shape
    contract = (((1,), (1,)), ((), ()))

    def kernel(far, *refs):
        far_in, far_out = refs[:5], refs[6]
        near, gather, expand, wg, wu, wd = refs[7:13]
        x, cot, d_gate, d_up, made, rest, extra, last, stacked, sems = refs[13:]
        tables = (gather, expand)
        parts = load_all(
            [far.at[:, pl.ds(u * LANES, LANES)] for u in range(2)],
            [near.at[:, pl.ds(u * LANES, LANES)] for u in range(2)],
            sems,
        )
        loads = load_all(far_in, (gather, expand, wg, wu, wd), sems, 2)
        for load in (parts[0], loads[0], loads[1], parts[1], *loads[2:]):
            load.start()
        parts[0].wait()
        loads[0].wait()
        loads[1].wait()
        unpack(near, 0, tables, x, 0, last, stacked)
        parts[1].wait()
        unpack(near, LANES, tables, cot, 0, last, stacked)
        for load in loads[2:]:
            load.wait()

        def step(k, inner):
            cols = pl.ds(pl.multiple_of(k * 256, 256), 256)
            gate = jnp.dot(x[...], wg[:, cols], preferred_element_type=jnp.float32)
            upper = jnp.dot(x[...], wu[:, cols], preferred_element_type=jnp.float32)
            d_hidden = lax.dot_general(
                cot[...], wd[cols, :], contract, preferred_element_type=jnp.float32
            )
            s = jax.nn.sigmoid(gate)
            active = gate * s
            value = f32((active * upper).astype(jnp.bfloat16))
            d_gate[:, cols] = (d_hidden * upper * s * (1.0 + gate * (1.0 - s))).astype(
                jnp.bfloat16
            )
            d_up[:, cols] = (d_hidden * active).astype(jnp.bfloat16)
            return inner + jnp.sum(value * d_hidden, axis=1, keepdims=True)

        inner = lax.fori_loop(0, units // 256, step, jnp.zeros((320, 1), jnp.float32))
        slot = lax.rem(lax.broadcasted_iota(jnp.int32, (320, 128), 0), CAP)
        lane = lax.broadcasted_iota(jnp.int32, (320, 128), 1)
        extra[...] = jnp.where(slot == lane, inner, 0.0).astype(jnp.bfloat16)

        def back(cols):
            return lax.dot_general(
                d_gate[...], wg[cols, :], contract, preferred_element_type=jnp.float32
            ) + lax.dot_general(
                d_up[...], wu[cols, :], contract, preferred_element_type=jnp.float32
            )

        put_result(made, rest, back)
        repack(near, 0, tables, made, rest, extra)
        store = pltpu.make_async_copy(near.at[:, pl.ds(0, LANES)], far_out, sems.at[7])
        store.start()
        store.wait()

    rows = chunks.shape[0]
    return pl.pallas_call(
        kernel,
        out_shape=jax.ShapeDtypeStruct((rows, LANES), jnp.bfloat16),
        in_specs=[FAR] * 6 + [pl.BlockSpec(memory_space=pl.ANY)],
        out_specs=FAR,
        scratch_shapes=[pltpu.VMEM((rows, 2 * LANES), jnp.bfloat16)]
        + [pltpu.VMEM(v.shape, v.dtype) for v in (*tables, *weights)]
        + [
            pltpu.VMEM((320, width), jnp.bfloat16),
            pltpu.VMEM((320, width), jnp.bfloat16),
            pltpu.VMEM((320, units), jnp.bfloat16),
            pltpu.VMEM((320, units), jnp.bfloat16),
            pltpu.VMEM((1024, LANES), jnp.bfloat16),
            pltpu.VMEM((320, 128), jnp.bfloat16),
            pltpu.VMEM((320, 128), jnp.bfloat16),
            pltpu.VMEM((64, LANES), jnp.bfloat16),
            pltpu.VMEM((320, 128), jnp.bfloat16),
            pltpu.SemaphoreType.DMA((8,)),
        ],
        **params(),
    )(chunks, *tables, *weights, after)


def spread_weights(weights, routes):
    tokens = routes[0].shape[1]
    total_rows = 64 * ROWS
    n = len(routes)

    def kernel(*refs):
        w_refs, id_refs, outs = refs[:n], refs[n : 2 * n], refs[2 * n :]
        square = (tokens, tokens)
        before = lax.broadcasted_iota(jnp.int32, square, 1) < lax.broadcasted_iota(
            jnp.int32, square, 0
        )
        shape = (tokens, total_rows)
        expert, row, block, slot = place_of(lax.broadcasted_iota(jnp.int32, shape, 1))
        place = lax.broadcasted_iota(jnp.int32, (tokens, 64 * CAP), 1)
        place = lax.bitwise_and(place, 31) * 8 + lax.shift_right_logical(place, 6)
        for at in range(n):
            w, ids = w_refs[at], f32(id_refs[at][...])
            first_r, second_r = ids[0:1, :], ids[1:2, :]
            first, second = as_column(first_r), as_column(second_r)
            slot_0 = count((first == first_r) & before, 1)
            slot_1 = count(second == first_r, 1) + count((second == second_r) & before, 1)
            key_0, key_1 = first * 8 + slot_0, second * 8 + slot_1

            def spread(key, w=w, key_0=key_0, key_1=key_1):
                key = f32(key)
                total = jnp.where(key_0 == key, w[:, 0:1], 0.0) + jnp.where(
                    key_1 == key, w[:, 1:2], 0.0
                )
                upper = f32(total.astype(jnp.bfloat16))
                return upper, total - upper

            for i, value in enumerate(spread(expert * 8 + slot)):
                for g in range(3):
                    start = 2 * tokens * g + tokens * i
                    outs[2 * at][start : start + tokens, :] = jnp.where(
                        block == g, value, 0.0
                    ).astype(jnp.bfloat16)
            for i, value in enumerate(spread(place)):
                outs[2 * at + 1][tokens * i : tokens * i + tokens, :] = value.astype(jnp.bfloat16)
            if at == n - 1:
                source = lax.broadcasted_iota(jnp.int32, (tokens, 64), 1)
                source = f32(lax.bitwise_and(source, 31))
                for k, (chosen, number) in enumerate(((first, slot_0), (second, slot_1))):
                    outs[2 * n][tokens * k : tokens * k + tokens, :] = jnp.where(
                        source == chosen, 1.0, 0.0
                    ).astype(jnp.bfloat16)
                    outs[2 * n + 1][:, 128 * k : 128 * k + 128] = jnp.broadcast_to(
                        number, (tokens, 128)
                    )

    shapes = [(6 * tokens, total_rows), (2 * tokens, 64 * CAP)] * n + [(2 * tokens, 64)]
    return pl.pallas_call(
        kernel,
        out_shape=[jax.ShapeDtypeStruct(shape, jnp.bfloat16) for shape in shapes]
        + [jax.ShapeDtypeStruct((tokens, 256), jnp.float32)],
        in_specs=[NEAR] * (2 * n),
        out_specs=[NEAR] * (2 * n + 2),
        **params(),
    )(*weights, *routes)


def last_rows(near, columns):
    shape = (64, 64 * ROWS)
    wanted = lax.broadcasted_iota(jnp.int32, shape, 0) * ROWS + (ROWS - 1)
    pick = jnp.where(wanted == lax.broadcasted_iota(jnp.int32, shape, 1), 1.0, 0.0)
    return jnp.dot(
        pick.astype(jnp.bfloat16), near[:, :columns], preferred_element_type=jnp.float32
    ).astype(jnp.bfloat16)


def add_up(near, rows_15, stacked, parts, tails, store):
    tokens = tails.shape[0] // 2
    for s in range(CAP):
        stacked[64 * s : 64 * s + 64, :] = rows_15[:, 128 * s : 128 * s + 128]
    rest = jnp.dot(tails[...], stacked[...], preferred_element_type=jnp.float32)
    store(TAIL, 128, rest[:tokens] + rest[tokens:])
    for c in range(3):
        part = jnp.dot(
            parts[...], near[:, 384 * c : 384 * c + 384], preferred_element_type=jnp.float32
        )
        for g in range(3):
            at = 2 * tokens * g
            store(
                g * LANES + 384 * c,
                384,
                part[at : at + tokens] + part[at + tokens : at + 2 * tokens],
            )


def finish_forward(chunks, parts, tails, rows):
    tokens, width = rows.shape
    operands = [parts, tails, rows]

    def kernel(near, *refs):
        out, held, result, stacked, sems = refs[3], refs[4:7], refs[7], refs[8], refs[9]
        parts, tails, v = held
        loads = load_all(refs[:3], held, sems)
        for load in loads:
            load.start()
        rows_15 = last_rows(near, 640)
        for load in loads:
            load.wait()

        def put(at, size, value):
            result[:, at : at + size] = (f32(v[:, at : at + size]) + value).astype(jnp.bfloat16)

        add_up(near, rows_15, stacked, parts, tails, put)
        store = pltpu.make_async_copy(result, out, sems.at[3])
        store.start()
        store.wait()

    return pl.pallas_call(
        kernel,
        out_shape=jax.ShapeDtypeStruct((tokens, width), jnp.bfloat16),
        in_specs=[NEAR] + [FAR] * 3,
        out_specs=FAR,
        scratch_shapes=[pltpu.VMEM(v.shape, v.dtype) for v in operands]
        + [
            pltpu.VMEM((tokens, width), jnp.bfloat16),
            pltpu.VMEM((64 * CAP, 128), jnp.bfloat16),
            pltpu.SemaphoreType.DMA((4,)),
        ],
        **params(),
    )(chunks, *operands)


def finish_backward(chunks, spreads, rows, cotangent, routes, picked, gain, router_rows):
    tokens, width = rows.shape
    operands = [*spreads, rows, cotangent, routes, picked, gain, router_rows]
    n = len(operands)

    def kernel(near, *refs):
        out, held = refs[n], refs[n + 1 : 2 * n + 1]
        gradient, total, stacked, sems = refs[2 * n + 1 :]
        parts, tails, picks, slots, v_ref, cot, ids, chosen, gain_ref, router_ref = held
        loads = load_all(refs[:n], held, sems)
        for load in loads:
            load.start()
        rows_15 = last_rows(near, 768)
        for load in loads:
            load.wait()
        found = jnp.dot(picks[...], rows_15[:, 640:], preferred_element_type=jnp.float32)
        lane = f32(lax.broadcasted_iota(jnp.int32, (tokens, 128), 1))
        inner = [
            jnp.sum(
                jnp.where(
                    lane == slots[:, 128 * k : 128 * k + 128],
                    found[tokens * k : tokens * k + tokens],
                    0.0,
                ),
                axis=1,
                keepdims=True,
            )
            for k in range(2)
        ]
        scores = [chosen[:, k : k + 1] for k in range(2)]
        whole = scores[0] + scores[1]
        mean = (inner[0] * scores[0] + inner[1] * scores[1]) / whole
        numbers = f32(ids[...])
        numbers = [as_column(numbers[k : k + 1, :]) for k in range(2)]
        d_logits = jnp.zeros((tokens, 128), jnp.float32)
        for k in range(2):
            d_logit = (inner[k] - mean) / whole * scores[k] * (1.0 - scores[k])
            d_logits += jnp.where(lane == numbers[k], d_logit, 0.0)
        pieces, left = [], d_logits
        for _ in range(3):
            pieces.append(left.astype(jnp.bfloat16))
            left = left - f32(pieces[-1])
        pieces = jnp.concatenate(pieces, axis=0)

        def keep(at, size, value):
            routed = jnp.dot(
                pieces, router_ref[:, at : at + size], preferred_element_type=jnp.float32
            )
            for i in range(3):
                value += routed[tokens * i : tokens * i + tokens]
            total[:, at : at + size] = value * gain_ref[:, at : at + size]

        add_up(near, rows_15, stacked, parts, tails, keep)
        v = f32(v_ref[...])
        inverse = lax.rsqrt(jnp.mean(v * v, axis=-1, keepdims=True) + epsilon)
        projected = jnp.mean(v * total[...], axis=-1, keepdims=True)
        d_rows = total[...] * inverse - v * (inverse * inverse * inverse * projected)
        gradient[...] = (f32(cot[...]) + d_rows).astype(jnp.bfloat16)
        store = pltpu.make_async_copy(gradient, out, sems.at[n])
        store.start()
        store.wait()

    return pl.pallas_call(
        kernel,
        out_shape=jax.ShapeDtypeStruct((tokens, width), jnp.bfloat16),
        in_specs=[NEAR] + [FAR] * n,
        out_specs=FAR,
        scratch_shapes=[pltpu.VMEM(v.shape, v.dtype) for v in operands]
        + [
            pltpu.VMEM((tokens, width), jnp.bfloat16),
            pltpu.VMEM((tokens, width), jnp.float32),
            pltpu.VMEM((64 * CAP, 128), jnp.bfloat16),
            pltpu.SemaphoreType.DMA((n + 1,)),
        ],
        **params(),
    )(chunks, *operands)


def swapped(chunks):
    shape = chunks.shape
    chunks = chunks.reshape(shape[0] // ROWS, ROWS, shape[1])
    return lax.all_to_all(chunks, "expert", 0, 0, tiled=True).reshape(shape)


def passed_along(x, axis, by):
    n = lax.axis_size(axis)
    return lax.ppermute(x, axis, [(i, (i + by) % n) for i in range(n)])


def normalise(values, gain_row):
    inverse = lax.rsqrt(jnp.mean(values * values, axis=-1, keepdims=True) + epsilon)
    return values * inverse * gain_row


def picked_scores(values, gain_row, router_map, routes):
    normed = normalise(values.astype(jnp.float32), gain_row)
    logits = jnp.dot(normed, router_map.astype(jnp.float32), precision=lax.Precision.HIGHEST)
    scores = jax.nn.sigmoid(logits)
    choices_axis = jnp.arange(router_map.shape[1], dtype=jnp.int32)
    onehot = (routes[:, :, None] == choices_axis[None, None, :]).astype(scores.dtype)
    return jnp.sum(onehot * scores[:, None, :], axis=-1)


def body(
    forward_rows,
    forward_routes,
    saved_rows,
    cotangent,
    backward_routes,
    norm_gain,
    router,
    gate_weight,
    up_weight,
    down_weight,
):
    gain_row, router_map = norm_gain[0], router[0]
    weights = (gate_weight[0, 0], up_weight[0, 0], down_weight[0, 0])
    tables = selections()
    backward_ids, forward_ids = backward_routes[0], forward_routes[0]

    backward_names, forward_names = backward_ids.T, forward_ids.T
    saved, cotan, forward = saved_rows[0], cotangent[0], forward_rows[0]

    sent = pack(
        [(saved, True, 0), (cotan, False, 0), (forward, True, 1)],
        norm_gain,
        [backward_names, forward_names],
    )
    received = swapped(sent)
    backward_scores = picked_scores(saved, gain_row, router_map, backward_ids)
    forward_scores = picked_scores(forward, gain_row, router_map, forward_ids)
    spreads = spread_weights(
        [v / jnp.sum(v, axis=1, keepdims=True) for v in (forward_scores, backward_scores)],
        [forward_names, backward_names],
    )
    forward_chunks = experts_forward(received, 2 * LANES, tables, weights)
    backward_chunks = experts_backward(received, tables, weights, forward_chunks)
    forward_back, backward_back = swapped(forward_chunks), swapped(backward_chunks)
    router_rows = jnp.pad(router_map.T, ((0, 128 - router_map.shape[1]), (0, 0)))
    result = finish_forward(forward_back, spreads[0], spreads[1], forward)
    result, _ = lax.optimization_barrier((result, backward_back))
    gradient = finish_backward(
        backward_back,
        spreads[2:],
        saved,
        cotan,
        backward_names,
        backward_scores,
        norm_gain,
        router_rows,
    )
    backward_next = passed_along(gradient[None], "pipe", -1)
    forward_next = passed_along(result[None], "pipe", 1)
    return (forward_next, backward_next)


def solution(mesh):
    in_specs = (
        P("pipe", "expert", None),
        P("pipe", "expert", None),
        P("pipe", "expert", None),
        P("pipe", "expert", None),
        P("pipe", "expert", None),
        P("pipe", None),
        P("pipe", None, None),
        P("pipe", "expert", None, None),
        P("pipe", "expert", None, None),
        P("pipe", "expert", None, None),
    )
    out_specs = (P("pipe", "expert", None), P("pipe", "expert", None))
    return jax.shard_map(body, mesh=mesh, in_specs=in_specs, out_specs=out_specs, check_vma=False)
```

```python
import jax
import jax.numpy as jnp
import numpy as np
from jax import lax
from jax.experimental import pallas as pl
from jax.experimental.pallas import tpu as pltpu
from jax.sharding import PartitionSpec as P

epsilon = 1e-06
VMEM_LIMIT = 63 * 1024 * 1024 + 512 * 1024
CAP = 5
LANES = 1152
ROWS = 16
TAIL = 3 * LANES
FAR = pl.BlockSpec(memory_space=pltpu.HBM)
NEAR = pl.BlockSpec(memory_space=pltpu.VMEM)


def selections():
    gather = np.zeros((256, 256), np.float32)
    for i in range(16):
        gather[240 + i, 16 * i + 15] = 1
        for s in range(CAP):
            for g in range(3):
                gather[80 * g + CAP * i + s, 16 * i + 5 * g + s] = 1
    expand = np.zeros((320, 320), np.float32)
    for i in range(64):
        for s in range(CAP):
            expand[CAP * i + s, 64 * s + i] = 1
    whole = expand.reshape(320, CAP, 64).sum(1)
    chunks = np.concatenate([gather, gather.T])
    slots = np.concatenate([expand, expand.T, whole.T])
    return jnp.asarray(chunks, jnp.bfloat16), jnp.asarray(slots, jnp.bfloat16)


def params():
    return dict(
        compiler_params=pltpu.CompilerParams(vmem_limit_bytes=VMEM_LIMIT),
        cost_estimate=pl.CostEstimate(flops=0, bytes_accessed=1024, transcendentals=0),
    )


def f32(x):
    return x.astype(jnp.float32)


def count(hits, axis):
    return jnp.sum(jnp.where(hits, 1.0, 0.0), axis=axis, keepdims=True)


def place_of(position):
    expert = lax.bitwise_and(lax.shift_right_logical(position, 4), 31)
    row = lax.bitwise_and(position, 15)
    block = jnp.where(row >= 5, 1, 0) + jnp.where(row >= 10, 1, 0) + jnp.where(row >= 15, 1, 0)
    return expert, row, block, row - 5 * block


def as_row(column, copies):
    n = column.shape[0]
    shape = (n, copies * n)
    lane = lax.bitwise_and(lax.broadcasted_iota(jnp.int32, shape, 1), n - 1)
    hit = lax.broadcasted_iota(jnp.int32, shape, 0) == lane
    return jnp.sum(jnp.where(hit, column, 0.0), axis=0, keepdims=True)


def as_column(row):
    shape = (row.shape[1], row.shape[1])
    hit = lax.broadcasted_iota(jnp.int32, shape, 0) == lax.broadcasted_iota(jnp.int32, shape, 1)
    return jnp.sum(jnp.where(hit, row, 0.0), axis=1, keepdims=True)


def pack(units, gain, routes):
    n, m = len(units), len(routes)
    tokens, width = units[0][0].shape
    half_rows = 32 * ROWS
    operands = [*routes, gain, *[rows for rows, _, _ in units]]

    def kernel(*refs):
        far, out = refs[: n + m + 1], refs[n + m + 1]
        near = refs[n + m + 2 : 2 * (n + m) + 3]
        made, stacked, sems = refs[2 * (n + m) + 3 :]
        loads = [
            pltpu.make_async_copy(src, dst, sems.at[i]) for i, (src, dst) in enumerate(zip(far, near))
        ]
        for load in loads:
            load.start()
        for load in loads[: m + 1]:
            load.wait()
        gain_ref = near[m]
        shape = (half_rows, 4 * tokens)
        expert, row, block, slot = place_of(lax.broadcasted_iota(jnp.int32, shape, 0))
        lane = lax.broadcasted_iota(jnp.int32, shape, 1)
        body_lanes = (lane < 3 * tokens) & (block == lax.shift_right_logical(lane, 6))
        tail_lanes = (row == 15) & (lane == 3 * tokens + expert)
        place = lax.broadcasted_iota(jnp.int32, (32 * CAP, tokens), 0)
        tail_key = lax.bitwise_and(place, 31) * 8 + lax.shift_right_logical(place, 5)
        stores = []
        stacked[3 * tokens :, :] = jnp.zeros((tokens, LANES), jnp.bfloat16)
        for route in range(m):
            ids = f32(near[route][...])
            first, second = as_column(ids[0:1, :]), as_column(ids[1:2, :])
            first_r, second_r = as_row(first, 4), as_row(second, 4)
            square = (tokens, 4 * tokens)
            other = lax.bitwise_and(lax.broadcasted_iota(jnp.int32, square, 1), tokens - 1)
            before = lax.broadcasted_iota(jnp.int32, square, 0) < other
            slot_0 = count((first == first_r) & before, 0)
            slot_1 = count(first == second_r, 0) + count((second == second_r) & before, 0)
            key_0, key_1 = first_r * 8 + slot_0, second_r * 8 + slot_1
            key = f32(expert * 8 + slot)
            own = ((key_0 == key) | (key_1 == key)) & body_lanes
            pick = jnp.where(own | tail_lanes, 1.0, 0.0).astype(jnp.bfloat16)
            key = f32(tail_key)
            hit = (key_0[:, :tokens] == key) | (key_1[:, :tokens] == key)
            pick_tail = jnp.where(hit, 1.0, 0.0).astype(jnp.bfloat16)
            for u in range(n):
                if units[u][2] != route:
                    continue
                loads[m + 1 + u].wait()
                x = near[m + 1 + u][...]
                if units[u][1]:
                    v = f32(x)
                    inverse = lax.rsqrt(jnp.mean(v * v, axis=-1, keepdims=True) + epsilon)
                    x = (v * inverse * gain_ref[...]).astype(jnp.bfloat16)
                for g in range(3):
                    stacked[tokens * g : tokens * g + tokens, :] = x[:, g * LANES : (g + 1) * LANES]
                tail = jnp.dot(
                    pick_tail, x[:, TAIL:], preferred_element_type=jnp.float32
                ).astype(jnp.bfloat16)
                for s in range(CAP):
                    stacked[3 * tokens : 3 * tokens + 32, 128 * s : 128 * s + 128] = tail[
                        32 * s : 32 * s + 32
                    ]
                for c in range(3):
                    at = u * LANES + 384 * c
                    made[:, at : at + 384] = jnp.dot(
                        pick,
                        stacked[:, 384 * c : 384 * c + 384],
                        preferred_element_type=jnp.float32,
                    ).astype(jnp.bfloat16)
                lanes = pl.ds(u * LANES, LANES)
                for r in range(2):
                    stores.append(
                        pltpu.make_async_copy(
                            made.at[:, lanes],
                            out.at[pl.ds(half_rows * r, half_rows), lanes],
                            sems.at[n + m + 1 + 2 * u + r],
                        )
                    )
                    stores[-1].start()
        for store in stores:
            store.wait()

    return pl.pallas_call(
        kernel,
        out_shape=jax.ShapeDtypeStruct((2 * half_rows, n * LANES), jnp.bfloat16),
        in_specs=[FAR] * (n + m + 1),
        out_specs=FAR,
        scratch_shapes=[pltpu.VMEM(v.shape, v.dtype) for v in operands]
        + [
            pltpu.VMEM((half_rows, n * LANES), jnp.bfloat16),
            pltpu.VMEM((4 * tokens, LANES), jnp.bfloat16),
            pltpu.SemaphoreType.DMA((3 * n + m + 1,)),
        ],
        **params(),
    )(*operands)


def unpack(chunks, offset, tables, x, start, last, stacked):
    gather, expand = tables

    for b in range(4):
        held = slice(256 * b, 256 * b + 256)
        rows = slice(start + 80 * b, start + 80 * b + 80)
        for c in range(3):
            part = jnp.dot(
                gather[:256, :],
                chunks[held, offset + 384 * c : offset + 384 * c + 384],
                preferred_element_type=jnp.float32,
            ).astype(jnp.bfloat16)
            for g in range(3):
                at = g * LANES + 384 * c
                x[rows, at : at + 384] = part[80 * g : 80 * g + 80]
            last[16 * b : 16 * b + 16, 384 * c : 384 * c + 384] = part[240:]
    for s in range(CAP):
        stacked[64 * s : 64 * s + 64, :] = last[:, 128 * s : 128 * s + 128]
    x[start : start + 320, TAIL:] = jnp.dot(
        expand[:320, :], stacked[...], preferred_element_type=jnp.float32
    ).astype(jnp.bfloat16)


def repack(chunks, offset, tables, made, rest, extra=None, stores=()):
    gather, expand = tables
    tail = jnp.dot(
        expand[320:640, :], rest[...], preferred_element_type=jnp.float32
    ).astype(jnp.bfloat16)
    spare = jnp.zeros((64, 128), jnp.bfloat16)
    if extra is not None:
        spare = jnp.dot(
            expand[640:, :], extra[...], preferred_element_type=jnp.float32
        ).astype(jnp.bfloat16)
    for b in range(4):
        at = slice(256 * b + 240, 256 * b + 256)
        for s in range(CAP):
            made[at, 128 * s : 128 * s + 128] = tail[64 * s + 16 * b : 64 * s + 16 * b + 16]
        made[at, 640:768] = spare[16 * b : 16 * b + 16]
        made[at, 768:] = jnp.zeros((16, LANES - 768), jnp.bfloat16)

    for b in range(4):
        held = slice(256 * b, 256 * b + 256)
        chunks[held, offset : offset + LANES] = jnp.dot(
            gather[256:, :], made[held, :], preferred_element_type=jnp.float32
        ).astype(jnp.bfloat16)
        if stores:
            stores[b].start()
    for store in stores:
        store.wait()


def put_result(made, rest, product):
    for g in range(3):
        part = product(pl.ds(g * LANES, LANES)).astype(jnp.bfloat16)
        for b in range(4):
            made[256 * b + 80 * g : 256 * b + 80 * g + 80, :] = part[80 * b : 80 * b + 80]
    rest[...] = product(pl.ds(TAIL, 128)).astype(jnp.bfloat16)


def load_all(far, near, sems, first=0):
    return [
        pltpu.make_async_copy(src, dst, sems.at[first + n])
        for n, (src, dst) in enumerate(zip(far, near))
    ]


def experts_forward(chunks, offset, tables, weights):
    width, units = weights[0].shape
    half = units // 2

    def kernel(far, *refs):
        far_in, far_out = refs[:5], refs[5]
        near, gather, expand, wg, wu, wd, x, hidden, made, rest, last, stacked, sems = refs[6:]
        tables = (gather, expand)
        part = pltpu.make_async_copy(far.at[:, pl.ds(offset, LANES)], near, sems.at[0])
        loads = load_all(
            (far_in[0], far_in[1], far_in[4]), (gather, expand, wd), sems, 1
        )
        pieces = []
        for k in range(2):
            cols = pl.ds(half * k, half)
            pieces += load_all(
                (far_in[2].at[:, cols], far_in[3].at[:, cols]),
                (wg.at[:, cols], wu.at[:, cols]),
                sems,
                4 + 2 * k,
            )
        for load in (part, loads[0], loads[1], *pieces, loads[2]):
            load.start()
        part.wait()
        loads[0].wait()
        loads[1].wait()
        unpack(near, 0, tables, x, 0, last, stacked)
        for k in range(2):
            pieces[2 * k].wait()
            pieces[2 * k + 1].wait()
            cols = pl.ds(half * k, half)
            gate = jnp.dot(x[...], wg[:, cols], preferred_element_type=jnp.float32)
            upper = jnp.dot(x[...], wu[:, cols], preferred_element_type=jnp.float32)
            hidden[:, cols] = (gate * jax.nn.sigmoid(gate) * upper).astype(jnp.bfloat16)
        loads[2].wait()
        put_result(
            made,
            rest,
            lambda cols: jnp.dot(hidden[...], wd[:, cols], preferred_element_type=jnp.float32),
        )
        stores = [
            pltpu.make_async_copy(
                near.at[pl.ds(256 * b, 256)], far_out.at[pl.ds(256 * b, 256)], sems.at[8 + b]
            )
            for b in range(4)
        ]
        repack(near, 0, tables, made, rest, stores=stores)

    rows = chunks.shape[0]
    return pl.pallas_call(
        kernel,
        out_shape=jax.ShapeDtypeStruct((rows, LANES), jnp.bfloat16),
        in_specs=[FAR] * 6,
        out_specs=FAR,
        scratch_shapes=[pltpu.VMEM((rows, LANES), jnp.bfloat16)]
        + [pltpu.VMEM(v.shape, v.dtype) for v in (*tables, *weights)]
        + [
            pltpu.VMEM((320, width), jnp.bfloat16),
            pltpu.VMEM((320, units), jnp.bfloat16),
            pltpu.VMEM((1024, LANES), jnp.bfloat16),
            pltpu.VMEM((320, 128), jnp.bfloat16),
            pltpu.VMEM((64, LANES), jnp.bfloat16),
            pltpu.VMEM((320, 128), jnp.bfloat16),
            pltpu.SemaphoreType.DMA((12,)),
        ],
        **params(),
    )(chunks, *tables, *weights)


def experts_backward(chunks, tables, weights, after):
    width, units = weights[0].shape
    contract = (((1,), (1,)), ((), ()))

    def kernel(far, *refs):
        far_in, far_out = refs[:5], refs[6]
        near, gather, expand, wg, wu, wd = refs[7:13]
        x, cot, d_gate, d_up, made, rest, extra, last, stacked, sems = refs[13:]
        tables = (gather, expand)
        parts = load_all(
            [far.at[:, pl.ds(u * LANES, LANES)] for u in range(2)],
            [near.at[:, pl.ds(u * LANES, LANES)] for u in range(2)],
            sems,
        )
        loads = load_all(far_in, (gather, expand, wg, wu, wd), sems, 2)
        for load in (parts[0], loads[0], loads[1], parts[1], *loads[2:]):
            load.start()
        parts[0].wait()
        loads[0].wait()
        loads[1].wait()
        unpack(near, 0, tables, x, 0, last, stacked)
        parts[1].wait()
        unpack(near, LANES, tables, cot, 0, last, stacked)
        for load in loads[2:]:
            load.wait()

        def step(k, inner):
            cols = pl.ds(pl.multiple_of(k * 256, 256), 256)
            gate = jnp.dot(x[...], wg[:, cols], preferred_element_type=jnp.float32)
            upper = jnp.dot(x[...], wu[:, cols], preferred_element_type=jnp.float32)
            d_hidden = lax.dot_general(
                cot[...], wd[cols, :], contract, preferred_element_type=jnp.float32
            )
            s = jax.nn.sigmoid(gate)
            active = gate * s
            value = f32((active * upper).astype(jnp.bfloat16))
            d_gate[:, cols] = (d_hidden * upper * s * (1.0 + gate * (1.0 - s))).astype(
                jnp.bfloat16
            )
            d_up[:, cols] = (d_hidden * active).astype(jnp.bfloat16)
            return inner + jnp.sum(value * d_hidden, axis=1, keepdims=True)

        inner = lax.fori_loop(0, units // 256, step, jnp.zeros((320, 1), jnp.float32))
        slot = lax.rem(lax.broadcasted_iota(jnp.int32, (320, 128), 0), CAP)
        lane = lax.broadcasted_iota(jnp.int32, (320, 128), 1)
        extra[...] = jnp.where(slot == lane, inner, 0.0).astype(jnp.bfloat16)

        def back(cols):
            return lax.dot_general(
                d_gate[...], wg[cols, :], contract, preferred_element_type=jnp.float32
            ) + lax.dot_general(
                d_up[...], wu[cols, :], contract, preferred_element_type=jnp.float32
            )

        put_result(made, rest, back)
        repack(near, 0, tables, made, rest, extra)
        store = pltpu.make_async_copy(near.at[:, pl.ds(0, LANES)], far_out, sems.at[7])
        store.start()
        store.wait()

    rows = chunks.shape[0]
    return pl.pallas_call(
        kernel,
        out_shape=jax.ShapeDtypeStruct((rows, LANES), jnp.bfloat16),
        in_specs=[FAR] * 6 + [pl.BlockSpec(memory_space=pl.ANY)],
        out_specs=FAR,
        scratch_shapes=[pltpu.VMEM((rows, 2 * LANES), jnp.bfloat16)]
        + [pltpu.VMEM(v.shape, v.dtype) for v in (*tables, *weights)]
        + [
            pltpu.VMEM((320, width), jnp.bfloat16),
            pltpu.VMEM((320, width), jnp.bfloat16),
            pltpu.VMEM((320, units), jnp.bfloat16),
            pltpu.VMEM((320, units), jnp.bfloat16),
            pltpu.VMEM((1024, LANES), jnp.bfloat16),
            pltpu.VMEM((320, 128), jnp.bfloat16),
            pltpu.VMEM((320, 128), jnp.bfloat16),
            pltpu.VMEM((64, LANES), jnp.bfloat16),
            pltpu.VMEM((320, 128), jnp.bfloat16),
            pltpu.SemaphoreType.DMA((8,)),
        ],
        **params(),
    )(chunks, *tables, *weights, after)


def spread_weights(weights, routes):
    tokens = routes[0].shape[1]
    total_rows = 64 * ROWS
    n = len(routes)

    def kernel(*refs):
        w_refs, id_refs, outs = refs[:n], refs[n : 2 * n], refs[2 * n :]
        square = (tokens, tokens)
        before = lax.broadcasted_iota(jnp.int32, square, 1) < lax.broadcasted_iota(
            jnp.int32, square, 0
        )
        shape = (tokens, total_rows)
        expert, row, block, slot = place_of(lax.broadcasted_iota(jnp.int32, shape, 1))
        place = lax.broadcasted_iota(jnp.int32, (tokens, 64 * CAP), 1)
        place = lax.bitwise_and(place, 31) * 8 + lax.shift_right_logical(place, 6)
        for at in range(n):
            w, ids = w_refs[at], f32(id_refs[at][...])
            first_r, second_r = ids[0:1, :], ids[1:2, :]
            first, second = as_column(first_r), as_column(second_r)
            slot_0 = count((first == first_r) & before, 1)
            slot_1 = count(second == first_r, 1) + count((second == second_r) & before, 1)
            key_0, key_1 = first * 8 + slot_0, second * 8 + slot_1

            def spread(key, w=w, key_0=key_0, key_1=key_1):
                key = f32(key)
                total = jnp.where(key_0 == key, w[:, 0:1], 0.0) + jnp.where(
                    key_1 == key, w[:, 1:2], 0.0
                )
                upper = f32(total.astype(jnp.bfloat16))
                return upper, total - upper

            for i, value in enumerate(spread(expert * 8 + slot)):
                for g in range(3):
                    start = 2 * tokens * g + tokens * i
                    outs[2 * at][start : start + tokens, :] = jnp.where(
                        block == g, value, 0.0
                    ).astype(jnp.bfloat16)
            for i, value in enumerate(spread(place)):
                outs[2 * at + 1][tokens * i : tokens * i + tokens, :] = value.astype(jnp.bfloat16)
            if at == n - 1:
                source = lax.broadcasted_iota(jnp.int32, (tokens, 64), 1)
                source = f32(lax.bitwise_and(source, 31))
                for k, (chosen, number) in enumerate(((first, slot_0), (second, slot_1))):
                    outs[2 * n][tokens * k : tokens * k + tokens, :] = jnp.where(
                        source == chosen, 1.0, 0.0
                    ).astype(jnp.bfloat16)
                    outs[2 * n + 1][:, 128 * k : 128 * k + 128] = jnp.broadcast_to(
                        number, (tokens, 128)
                    )

    shapes = [(6 * tokens, total_rows), (2 * tokens, 64 * CAP)] * n + [(2 * tokens, 64)]
    return pl.pallas_call(
        kernel,
        out_shape=[jax.ShapeDtypeStruct(shape, jnp.bfloat16) for shape in shapes]
        + [jax.ShapeDtypeStruct((tokens, 256), jnp.float32)],
        in_specs=[NEAR] * (2 * n),
        out_specs=[NEAR] * (2 * n + 2),
        **params(),
    )(*weights, *routes)


def last_rows(near, columns):
    shape = (64, 64 * ROWS)
    wanted = lax.broadcasted_iota(jnp.int32, shape, 0) * ROWS + (ROWS - 1)
    pick = jnp.where(wanted == lax.broadcasted_iota(jnp.int32, shape, 1), 1.0, 0.0)
    return jnp.dot(
        pick.astype(jnp.bfloat16), near[:, :columns], preferred_element_type=jnp.float32
    ).astype(jnp.bfloat16)


def add_up(near, rows_15, stacked, parts, tails, store):
    tokens = tails.shape[0] // 2
    for s in range(CAP):
        stacked[64 * s : 64 * s + 64, :] = rows_15[:, 128 * s : 128 * s + 128]
    rest = jnp.dot(tails[...], stacked[...], preferred_element_type=jnp.float32)
    store(TAIL, 128, rest[:tokens] + rest[tokens:])
    for c in range(3):
        part = jnp.dot(
            parts[...], near[:, 384 * c : 384 * c + 384], preferred_element_type=jnp.float32
        )
        for g in range(3):
            at = 2 * tokens * g
            store(
                g * LANES + 384 * c,
                384,
                part[at : at + tokens] + part[at + tokens : at + 2 * tokens],
            )


def finish_forward(chunks, parts, tails, rows):
    tokens, width = rows.shape
    operands = [parts, tails, rows]

    def kernel(near, *refs):
        out, held, result, stacked, sems = refs[3], refs[4:7], refs[7], refs[8], refs[9]
        parts, tails, v = held
        loads = load_all(refs[:3], held, sems)
        for load in loads:
            load.start()
        rows_15 = last_rows(near, 640)
        for load in loads:
            load.wait()

        def put(at, size, value):
            result[:, at : at + size] = (f32(v[:, at : at + size]) + value).astype(jnp.bfloat16)

        add_up(near, rows_15, stacked, parts, tails, put)
        store = pltpu.make_async_copy(result, out, sems.at[3])
        store.start()
        store.wait()

    return pl.pallas_call(
        kernel,
        out_shape=jax.ShapeDtypeStruct((tokens, width), jnp.bfloat16),
        in_specs=[NEAR] + [FAR] * 3,
        out_specs=FAR,
        scratch_shapes=[pltpu.VMEM(v.shape, v.dtype) for v in operands]
        + [
            pltpu.VMEM((tokens, width), jnp.bfloat16),
            pltpu.VMEM((64 * CAP, 128), jnp.bfloat16),
            pltpu.SemaphoreType.DMA((4,)),
        ],
        **params(),
    )(chunks, *operands)


def finish_backward(chunks, spreads, rows, cotangent, routes, picked, gain, router_rows):
    tokens, width = rows.shape
    operands = [*spreads, rows, cotangent, routes, picked, gain, router_rows]
    n = len(operands)

    def kernel(far, *refs):
        out, held = refs[n], refs[n + 1 : 2 * n + 1]
        gradient, total, stacked, near, sems = refs[2 * n + 1 :]
        parts, tails, picks, slots, v_ref, cot, ids, chosen, gain_ref, router_ref = held
        loads = load_all(refs[:n], held, sems)
        chunk_load = pltpu.make_async_copy(far, near, sems.at[n + 1])
        small, large = (1, 2, 3, 4, 6, 7, 8), (9, 0, 5)
        for i in small:
            loads[i].start()
        chunk_load.start()
        for i in large:
            loads[i].start()
        for i in small:
            loads[i].wait()
        v = f32(v_ref[...])
        inverse = lax.rsqrt(jnp.mean(v * v, axis=-1, keepdims=True) + epsilon)
        chunk_load.wait()
        rows_15 = last_rows(near, 768)
        found = jnp.dot(picks[...], rows_15[:, 640:], preferred_element_type=jnp.float32)
        lane = f32(lax.broadcasted_iota(jnp.int32, (tokens, 128), 1))
        inner = [
            jnp.sum(
                jnp.where(
                    lane == slots[:, 128 * k : 128 * k + 128],
                    found[tokens * k : tokens * k + tokens],
                    0.0,
                ),
                axis=1,
                keepdims=True,
            )
            for k in range(2)
        ]
        scores = [chosen[:, k : k + 1] for k in range(2)]
        whole = scores[0] + scores[1]
        mean = (inner[0] * scores[0] + inner[1] * scores[1]) / whole
        numbers = f32(ids[...])
        numbers = [as_column(numbers[k : k + 1, :]) for k in range(2)]
        d_logits = jnp.zeros((tokens, 128), jnp.float32)
        for k in range(2):
            d_logit = (inner[k] - mean) / whole * scores[k] * (1.0 - scores[k])
            d_logits += jnp.where(lane == numbers[k], d_logit, 0.0)
        pieces, left = [], d_logits
        for _ in range(3):
            pieces.append(left.astype(jnp.bfloat16))
            left = left - f32(pieces[-1])
        pieces = jnp.concatenate(pieces, axis=0)[:, : router_ref.shape[0]]
        for i in large:
            loads[i].wait()

        def keep(at, size, value):
            routed = jnp.dot(
                pieces, router_ref[:, at : at + size], preferred_element_type=jnp.float32
            )
            for i in range(3):
                value += routed[tokens * i : tokens * i + tokens]
            total[:, at : at + size] = value * gain_ref[:, at : at + size]

        add_up(near, rows_15, stacked, parts, tails, keep)
        v = f32(v_ref[...])
        projected = jnp.mean(v * total[...], axis=-1, keepdims=True)
        d_rows = total[...] * inverse - v * (inverse * inverse * inverse * projected)
        gradient[...] = (f32(cot[...]) + d_rows).astype(jnp.bfloat16)
        store = pltpu.make_async_copy(gradient, out, sems.at[n])
        store.start()
        store.wait()

    return pl.pallas_call(
        kernel,
        out_shape=jax.ShapeDtypeStruct((tokens, width), jnp.bfloat16),
        in_specs=[FAR] * (n + 1),
        out_specs=FAR,
        scratch_shapes=[pltpu.VMEM(v.shape, v.dtype) for v in operands]
        + [
            pltpu.VMEM((tokens, width), jnp.bfloat16),
            pltpu.VMEM((tokens, width), jnp.float32),
            pltpu.VMEM((64 * CAP, 128), jnp.bfloat16),
            pltpu.VMEM(chunks.shape, jnp.bfloat16),
            pltpu.SemaphoreType.DMA((n + 2,)),
        ],
        **params(),
    )(chunks, *operands)


def swapped(chunks):
    shape = chunks.shape
    chunks = chunks.reshape(shape[0] // ROWS, ROWS, shape[1])
    return lax.all_to_all(chunks, "expert", 0, 0, tiled=True).reshape(shape)


def passed_along(x, axis, by):
    n = lax.axis_size(axis)
    return lax.ppermute(x, axis, [(i, (i + by) % n) for i in range(n)])


def normalise(values, gain_row):
    inverse = lax.rsqrt(jnp.mean(values * values, axis=-1, keepdims=True) + epsilon)
    return values * inverse * gain_row


def picked_scores(values, gain_row, router_map, routes):
    normed = normalise(values.astype(jnp.float32), gain_row)
    logits = jnp.dot(normed, router_map.astype(jnp.float32), precision=lax.Precision.HIGHEST)
    scores = jax.nn.sigmoid(logits)
    choices_axis = jnp.arange(router_map.shape[1], dtype=jnp.int32)
    onehot = (routes[:, :, None] == choices_axis[None, None, :]).astype(scores.dtype)
    return jnp.sum(onehot * scores[:, None, :], axis=-1)


def body(
    forward_rows,
    forward_routes,
    saved_rows,
    cotangent,
    backward_routes,
    norm_gain,
    router,
    gate_weight,
    up_weight,
    down_weight,
):
    gain_row, router_map = norm_gain[0], router[0]
    weights = (gate_weight[0, 0], up_weight[0, 0], down_weight[0, 0])
    tables = selections()
    backward_ids, forward_ids = backward_routes[0], forward_routes[0]

    backward_names, forward_names = backward_ids.T, forward_ids.T
    saved, cotan, forward = saved_rows[0], cotangent[0], forward_rows[0]

    sent = pack(
        [(saved, True, 0), (cotan, False, 0), (forward, True, 1)],
        norm_gain,
        [backward_names, forward_names],
    )
    received = swapped(sent)
    backward_scores = picked_scores(saved, gain_row, router_map, backward_ids)
    forward_scores = picked_scores(forward, gain_row, router_map, forward_ids)
    spreads = spread_weights(
        [v / jnp.sum(v, axis=1, keepdims=True) for v in (forward_scores, backward_scores)],
        [forward_names, backward_names],
    )
    forward_chunks = experts_forward(received, 2 * LANES, tables, weights)
    backward_chunks = experts_backward(received, tables, weights, forward_chunks)
    forward_back, backward_back = swapped(forward_chunks), swapped(backward_chunks)
    router_rows = router_map.T
    result = finish_forward(forward_back, spreads[0], spreads[1], forward)
    result, _ = lax.optimization_barrier((result, backward_back))
    gradient = finish_backward(
        backward_back,
        spreads[2:],
        saved,
        cotan,
        backward_names,
        backward_scores,
        norm_gain,
        router_rows,
    )
    backward_next = passed_along(gradient[None], "pipe", -1)
    forward_next = passed_along(result[None], "pipe", 1)
    return (forward_next, backward_next)


def solution(mesh):
    in_specs = (
        P("pipe", "expert", None),
        P("pipe", "expert", None),
        P("pipe", "expert", None),
        P("pipe", "expert", None),
        P("pipe", "expert", None),
        P("pipe", None),
        P("pipe", None, None),
        P("pipe", "expert", None, None),
        P("pipe", "expert", None, None),
        P("pipe", "expert", None, None),
    )
    out_specs = (P("pipe", "expert", None), P("pipe", "expert", None))
    return jax.shard_map(body, mesh=mesh, in_specs=in_specs, out_specs=out_specs, check_vma=False)
```
